32 devices in a mesh: cells: 8 (over z, x), tm: 4 (over y, core).
Axes of the slice: x: 2, y: 2, z: 4, core: 2. Of those that a mesh axis runs over, the one named last changes fastest.
Arguments:
- geopotential: bfloat16 [10240, 4096], P('tm', 'cells'), may hold values from -16 to 16
- meridional: bfloat16 [10240, 4096], P('tm', 'cells'), may hold values from -16 to 16
- day_index: int32 [10240], P('tm'), may hold values from 0 to 364, as said below
Outputs:
- eddy_climate: float32 [3, 365, 4096], P(None, None, 'cells')
- zonal_climate: float32 [3, 365, 128], replicated
The draws below stay inside these ranges and needn't reach their ends.
Inputs may be any that keep to these rules, and one draw needn't show every extreme that they name: `day_index`: consecutive daily frames of a calendar with a leap year every fourth year, in which February 29 shares the bin of February 28; every bin occurs.
All inputs are finite; a program needn't handle non-finite values.
Results may differ from the reference program's by a relative error of at most 0.00063.
The reference program's roundings to bfloat16 on the way count: a program that leaves them out, or rounds other values in their place, can miss the bound.
Values may be sent and summed in bfloat16 or wider, within the bound.
A program may use at most 128 MiB of HBM per device.

```python
import jax
import jax.numpy as jnp
from jax import lax

LAT = 128
HALF = 15
WIN = 7
DAYS = 365
C_DEV = 512
LON = 32
CELLS = 4096
TIMES = 10240


def common_parts(key):
    zonal_key, eddy_key, period_key, phase_key, amp_key = jax.random.split(key, 5)
    zonal_part = jax.random.normal(zonal_key, (TIMES, LAT), jnp.float32)
    shared_eddy = jax.random.normal(eddy_key, (TIMES, CELLS), jnp.float32)
    period = jax.random.randint(period_key, (CELLS,), 3, 8, jnp.int32)
    phase = jax.random.uniform(phase_key, (CELLS,), jnp.float32, -jnp.pi, jnp.pi)
    amp_unit = jax.random.uniform(amp_key, (CELLS,), jnp.float32, 0.0, 1.0)
    frame = jnp.arange(TIMES, dtype=jnp.int32)[:, None]
    cycle = (frame % period[None, :]).astype(jnp.float32) / period[None, :].astype(jnp.float32)
    wave = jnp.cos(2.0 * jnp.pi * cycle + phase[None, :])
    return (zonal_part, shared_eddy, wave, amp_unit)


def longitude_ramp(key):
    position = jnp.arange(LON, dtype=jnp.float32) / LON
    factor = jax.random.uniform(key, (LON,), jnp.float32, 0.7, 1.3)
    return jnp.repeat((1.0 + 2.0 * position) * factor, LAT)


def assemble(zonal_part, shared_eddy, private, ramp, strength, mixing, wave, amplitude):
    values = strength * jnp.tile(zonal_part, (1, LON)) * ramp[None, :] + mixing * shared_eddy + 0.7 * private
    values = values + amplitude[None, :] * wave
    return jnp.clip(values, -16.0, 16.0).astype(jnp.bfloat16)


def draw_geopotential(key, part):
    zonal_part, shared_eddy, wave, amp_unit = common_parts(key)
    key = jax.random.fold_in(key, 3)
    ramp_key, private_key = jax.random.split(key)
    private = jax.random.normal(private_key, (TIMES, CELLS), jnp.float32)
    strength = 2.0
    amplitude = 1.0 + 1.5 * amp_unit
    return assemble(zonal_part, shared_eddy, private, longitude_ramp(ramp_key), strength, 0.7, wave, amplitude)


def draw_meridional(key, part):
    zonal_part, shared_eddy, wave, amp_unit = common_parts(key)
    key = jax.random.fold_in(key, 5)
    ramp_key, private_key = jax.random.split(key)
    private = jax.random.normal(private_key, (TIMES, CELLS), jnp.float32)
    strength = 1.5
    amplitude = -(1.0 + 1.5 * amp_unit)
    return assemble(zonal_part, shared_eddy, private, longitude_ramp(ramp_key), strength, -0.7, wave, amplitude)


def draw_day_index(key, part):
    key = jax.random.fold_in(key, 7)
    anchor = jax.random.randint(key, (), 0, 1461, jnp.int32)
    elapsed = (anchor + jnp.arange(TIMES, dtype=jnp.int32)) % 1461
    leap_day = elapsed - 1095
    leap_bin = jnp.where(leap_day < 59, leap_day, leap_day - 1)
    return jnp.where(elapsed >= 1095, leap_bin, elapsed % 365).astype(jnp.int32)


def setup_inputs(seed: int = 0) -> dict:
    streams_of = jax.random.split(jax.random.key(seed), 4)
    geopotential = draw_geopotential(jax.random.fold_in(streams_of[3], 71), 0)
    meridional = draw_meridional(jax.random.fold_in(streams_of[3], 71), 0)
    day_index = draw_day_index(jax.random.fold_in(streams_of[3], 71), 0)
    return {"geopotential": geopotential, "meridional": meridional, "day_index": day_index}


def lanczos_tap(offset):
    nonzero = jnp.where(offset == 0, 1.0, offset)
    response = (jnp.sin(jnp.pi * nonzero) - jnp.sin(0.25 * jnp.pi * nonzero)) / (jnp.pi * nonzero)
    smoother = jnp.sin(jnp.pi * nonzero / (HALF + 1)) / (jnp.pi * nonzero / (HALF + 1))
    return jnp.where(offset == 0, 0.75, response * smoother)


def smooth_days(raw):
    total = jnp.zeros_like(raw)
    for shift_by in range(-WIN, WIN + 1):
        total = total + jnp.roll(raw, shift_by, axis=0)
    return total


def reference(geopotential, meridional, day_index):
    stacked = jnp.stack([geopotential, meridional])
    zonal_mean = jnp.sum(stacked.reshape(2, TIMES, LON, LAT), axis=2, dtype=jnp.float32) / LON
    taps = lanczos_tap(jnp.arange(-HALF, HALF + 1).astype(jnp.float32)).astype(jnp.bfloat16)
    taps = lax.optimization_barrier(taps).astype(jnp.float32)
    tallies = smooth_days(jax.ops.segment_sum(jnp.ones((TIMES,), jnp.float32), day_index, num_segments=DAYS))
    blocks = jnp.moveaxis(stacked.reshape(2, TIMES, CELLS // C_DEV, C_DEV), 2, 0)
    zonal_tiled = jnp.tile(zonal_mean, (1, 1, C_DEV // LAT))

    def one_block(frame_block):
        anomaly = (frame_block.astype(jnp.float32) - zonal_tiled).astype(jnp.bfloat16)
        anomaly = lax.optimization_barrier(anomaly).astype(jnp.float32)
        padded = jnp.pad(anomaly, ((0, 0), (HALF, HALF), (0, 0)))
        filtered = jnp.zeros((2, TIMES, C_DEV), jnp.float32)
        for tap_index in range(2 * HALF + 1):
            filtered = filtered + taps[tap_index] * padded[:, tap_index:tap_index + TIMES]
        height = filtered[0]
        meridional_f = filtered[1]
        products = jnp.stack([height * height, meridional_f * meridional_f, height * meridional_f]).astype(jnp.bfloat16)
        products = lax.optimization_barrier(products).astype(jnp.float32)
        raw = jax.ops.segment_sum(jnp.moveaxis(products, 1, 0), day_index, num_segments=DAYS)
        smoothed = smooth_days(raw)
        return jnp.moveaxis(smoothed, 0, 1) / tallies[None, :, None]

    climate = lax.map(one_block, blocks)
    climate = jnp.moveaxis(climate, 0, 2).reshape(3, DAYS, CELLS)
    zonal_climate = jnp.sum(climate.reshape(3, DAYS, LON, LAT), axis=2) / LON
    return (climate, zonal_climate)
```

```python
import functools

import jax
import jax.numpy as jnp
import numpy as np
from jax import lax
from jax.experimental import pallas as pl
from jax.experimental.pallas import tpu as pltpu
from jax.sharding import PartitionSpec as P

LAT = 128
HALF = 15
WIN = 7
DAYS = 365
DROWS = 384
EDGE = 16
TILE = 128
SLAB = TILE + 2 * EDGE
LIMIT = 48 * 1024 * 1024
MESH = pl.DeviceIdType.MESH
F32 = jnp.float32
BF16 = jnp.bfloat16


def vmem():
    return pl.BlockSpec(memory_space=pltpu.VMEM)


def taps_matrix():
    k = np.arange(SLAB)[None, :] - np.arange(TILE)[:, None] - EDGE
    x = np.where(k == 0, 1.0, k).astype(np.float64)
    response = (np.sin(np.pi * x) - np.sin(0.25 * np.pi * x)) / (np.pi * x)
    smoother = np.sin(np.pi * x / (HALF + 1)) / (np.pi * x / (HALF + 1))
    w = np.where(k == 0, 0.75, response * smoother)
    return jnp.asarray(np.where(np.abs(k) <= HALF, w, 0.0).astype(np.float32)).astype(BF16)


def lane_sum(block):
    total = block[:, :LAT].astype(F32)
    for start in range(LAT, block.shape[1], LAT):
        total = total + block[:, start : start + LAT].astype(F32)
    return total


def mean_kernel(n, rows_f, lon_total, geo, mer, halo, mean, part, inbox, ssem, rsem, gssem, grsem):
    me = lax.axis_index("cells")
    frames = geo.shape[0]
    share = part.shape[0] // n
    barrier = pltpu.get_barrier_semaphore()
    for k in range(1, n):
        pl.semaphore_signal(barrier, inc=1, device_id={"cells": lax.rem(me + k, n)}, device_id_type=MESH)

    for f, ref in enumerate((geo, mer)):

        @pl.loop(0, frames // 256)
        def _(i):
            r = pl.multiple_of(i * 256, 256)
            part[pl.ds(f * rows_f + r, 256), :] = lane_sum(ref[pl.ds(r, 256), :]).astype(BF16)

        base = f * rows_f + frames
        part[base : base + 2 * EDGE, :] = lane_sum(halo[f]).astype(BF16)
        rest = rows_f - frames - 2 * EDGE
        if rest:
            part[base + 2 * EDGE : base + 2 * EDGE + rest, :] = jnp.zeros((rest, LAT), BF16)

    pl.semaphore_wait(barrier, n - 1)
    copies = []
    for k in range(1, n):
        peer = lax.rem(me + k, n)
        copy = pltpu.make_async_remote_copy(
            src_ref=part.at[pl.ds(pl.multiple_of(peer * share, 16), share)],
            dst_ref=inbox.at[k - 1],
            send_sem=ssem.at[k - 1],
            recv_sem=rsem.at[k - 1],
            device_id={"cells": peer},
            device_id_type=MESH,
        )
        copy.start()
        copies.append(copy)
    mine = pl.ds(pl.multiple_of(me * share, 16), share)
    total = part[mine, :].astype(F32)
    for k in range(1, n):
        copies[k - 1].wait_recv()
        total = total + inbox[k - 1].astype(F32)
    mean[mine, :] = total / lon_total
    gathers = []
    for k in range(1, n):
        peer = lax.rem(me + k, n)
        copy = pltpu.make_async_remote_copy(
            src_ref=mean.at[mine],
            dst_ref=mean.at[mine],
            send_sem=gssem.at[k - 1],
            recv_sem=grsem.at[k - 1],
            device_id={"cells": peer},
            device_id_type=MESH,
        )
        copy.start()
        gathers.append(copy)
    for k in range(1, n):
        copies[k - 1].wait_send()
        gathers[k - 1].wait_send()
        source = lax.rem(me + n - k, n)
        theirs = mean.at[pl.ds(pl.multiple_of(source * share, 16), share)]
        pltpu.make_async_remote_copy(
            src_ref=theirs,
            dst_ref=theirs,
            send_sem=gssem.at[k - 1],
            recv_sem=grsem.at[k - 1],
            device_id={"cells": source},
            device_id_type=MESH,
        ).wait_recv()


def day_kernel(rows_f, geo, mer, halo, mean, days, taps, raw, padded, products, onehot):
    frames, width = geo.shape
    lons = width // LAT

    def put(field, dst, block, m):
        for j in range(lons):
            cols = slice(field * width + j * LAT, field * width + (j + 1) * LAT)
            padded[dst, cols] = (block[:, j * LAT : (j + 1) * LAT].astype(F32) - m).astype(BF16)

    for f, ref in enumerate((geo, mer)):
        base = f * rows_f + frames
        put(f, slice(0, EDGE), halo[f, :EDGE], mean[base : base + EDGE, :])
        put(f, slice(frames + EDGE, frames + 2 * EDGE), halo[f, EDGE:], mean[base + EDGE : base + 2 * EDGE, :])

        @pl.loop(0, frames // 128)
        def _(i):
            r = pl.multiple_of(i * 128, 128)
            put(f, pl.ds(r + EDGE, 128), ref[pl.ds(r, 128), :], mean[pl.ds(f * rows_f + r, 128), :])

    @pl.loop(0, frames // TILE)
    def _(i):
        r = pl.multiple_of(i * TILE, TILE)
        hit = lax.broadcasted_iota(jnp.int32, (DROWS, TILE), 0) == days[:, pl.ds(r, TILE)]
        onehot[:, pl.ds(r, TILE)] = jnp.where(hit, 1.0, 0.0).astype(BF16)
        for j in range(width // 256):
            lo, hi = j * 256, (j + 1) * 256
            a = jnp.dot(taps[...], padded[pl.ds(r, SLAB), lo:hi], preferred_element_type=F32)
            b = jnp.dot(taps[...], padded[pl.ds(r, SLAB), width + lo : width + hi], preferred_element_type=F32)
            products[pl.ds(r, TILE), lo:hi] = (a * a).astype(BF16)
            products[pl.ds(r, TILE), width + lo : width + hi] = (b * b).astype(BF16)
            products[pl.ds(r, TILE), 2 * width + lo : 2 * width + hi] = (a * b).astype(BF16)

    for s in range(3):

        @pl.loop(0, width // 256)
        def _(j):
            c = pl.multiple_of(j * 256, 256)
            raw[s * DROWS : (s + 1) * DROWS, pl.ds(c, 256)] = jnp.dot(
                onehot[...], products[:, pl.ds(s * width + c, 256)], preferred_element_type=F32
            )


def climate_kernel(
    n, zrows, lon_total, raw, tally, climate, zonal, inbox, own, other, zpart, zbox, sems, zsend, zrecv, gsend, grecv, tsend, trecv
):
    me = lax.axis_index("cells")
    tm = lax.axis_index("tm")
    core = lax.rem(tm, 2)
    partner = tm + 1 - 2 * core
    across = lax.rem(tm + 2, 4)
    half = raw.shape[1] // 2
    share = zrows // n
    barrier = pltpu.get_barrier_semaphore()
    for k in range(1, n):
        pl.semaphore_signal(barrier, inc=1, device_id={"cells": lax.rem(me + k, n)}, device_id_type=MESH)
    for k in range(1, 4):
        pl.semaphore_signal(barrier, inc=1, device_id={"tm": lax.rem(tm + k, 4)}, device_id_type=MESH)
    pl.semaphore_wait(barrier, n + 2)

    mine = pl.ds(pl.multiple_of(core * half, 128), half)
    theirs = pl.ds(pl.multiple_of((1 - core) * half, 128), half)
    first = pltpu.make_async_remote_copy(
        src_ref=raw.at[:, theirs], dst_ref=inbox, send_sem=sems.at[0], recv_sem=sems.at[1],
        device_id={"tm": partner}, device_id_type=MESH,
    )
    first.start()
    first.wait()
    own[...] = (raw[:, mine] + inbox[...]).astype(BF16)
    second = pltpu.make_async_remote_copy(
        src_ref=own, dst_ref=other, send_sem=sems.at[2], recv_sem=sems.at[3],
        device_id={"tm": across}, device_id_type=MESH,
    )
    second.start()
    d = lax.broadcasted_iota(jnp.int32, (DROWS, DROWS), 0)
    e = lax.broadcasted_iota(jnp.int32, (DROWS, DROWS), 1)
    gap = jnp.abs(d - e)
    inside = ((gap <= WIN) | (gap >= DAYS - WIN)) & (e < DAYS)
    window = jnp.where(inside, 1.0, 0.0).astype(BF16)
    for s in range(3):
        rows = slice(s * DROWS, (s + 1) * DROWS)
        inbox[rows, :] = jnp.dot(window, own[rows, :], preferred_element_type=F32)
    second.wait()
    for s in range(3):
        rows = slice(s * DROWS, (s + 1) * DROWS)
        total = inbox[rows, :] + jnp.dot(window, other[rows, :], preferred_element_type=F32)
        for j in range(half // LAT):
            cols = pl.ds(pl.multiple_of(core * half + j * LAT, 128), LAT)
            climate[rows, cols] = total[:, j * LAT : (j + 1) * LAT] / tally[...]
    third = pltpu.make_async_remote_copy(
        src_ref=climate.at[:, mine], dst_ref=climate.at[:, mine], send_sem=sems.at[4], recv_sem=sems.at[5],
        device_id={"tm": partner}, device_id_type=MESH,
    )
    third.start()
    third.wait_send()
    pltpu.make_async_remote_copy(
        src_ref=climate.at[:, theirs], dst_ref=climate.at[:, theirs], send_sem=sems.at[4], recv_sem=sems.at[5],
        device_id={"tm": partner}, device_id_type=MESH,
    ).wait_recv()

    quarter = climate.shape[0] // 4
    q = pl.multiple_of(tm * quarter, 8)
    zpart[:quarter, :] = lane_sum(climate[pl.ds(q, quarter), :])
    if zrows > quarter:
        zpart[quarter:, :] = jnp.zeros((zrows - quarter, LAT), F32)
    copies = []
    for k in range(1, n):
        peer = lax.rem(me + k, n)
        copy = pltpu.make_async_remote_copy(
            src_ref=zpart.at[pl.ds(pl.multiple_of(peer * share, 8), share)],
            dst_ref=zbox.at[k - 1], send_sem=zsend.at[k - 1], recv_sem=zrecv.at[k - 1],
            device_id={"cells": peer}, device_id_type=MESH,
        )
        copy.start()
        copies.append(copy)
    block = pl.ds(pl.multiple_of(me * share, 8), share)
    total = zpart[block, :]
    for k in range(1, n):
        copies[k - 1].wait_recv()
        total = total + zbox[k - 1]
    zonal[tm, block, :] = total / lon_total
    gathers = []
    for k in range(1, n):
        copy = pltpu.make_async_remote_copy(
            src_ref=zonal.at[tm, block], dst_ref=zonal.at[tm, block],
            send_sem=gsend.at[k - 1], recv_sem=grecv.at[k - 1],
            device_id={"cells": lax.rem(me + k, n)}, device_id_type=MESH,
        )
        copy.start()
        gathers.append(copy)
    for k in range(1, n):
        copies[k - 1].wait_send()
        gathers[k - 1].wait_send()
        source = lax.rem(me + n - k, n)
        there = zonal.at[tm, pl.ds(pl.multiple_of(source * share, 8), share)]
        pltpu.make_async_remote_copy(
            src_ref=there, dst_ref=there, send_sem=gsend.at[k - 1], recv_sem=grecv.at[k - 1],
            device_id={"cells": source}, device_id_type=MESH,
        ).wait_recv()
    spreads = []
    for k in range(1, 4):
        copy = pltpu.make_async_remote_copy(
            src_ref=zonal.at[tm], dst_ref=zonal.at[tm],
            send_sem=tsend.at[k - 1], recv_sem=trecv.at[k - 1],
            device_id={"tm": lax.rem(tm + k, 4)}, device_id_type=MESH,
        )
        copy.start()
        spreads.append(copy)
    for k in range(1, 4):
        spreads[k - 1].wait_send()
        source = lax.rem(tm + 4 - k, 4)
        pltpu.make_async_remote_copy(
            src_ref=zonal.at[source], dst_ref=zonal.at[source],
            send_sem=tsend.at[k - 1], recv_sem=trecv.at[k - 1],
            device_id={"tm": source}, device_id_type=MESH,
        ).wait_recv()


def local(geopotential, meridional, day_index):
    frames, width = geopotential.shape
    n = lax.axis_size("cells")
    size = lax.axis_size("tm")
    lon_total = width // LAT * n
    step = 8 * n
    rows_f = -(-(frames + 2 * EDGE) // step) * step
    share = 2 * rows_f // n

    up = [(i, i + 1) for i in range(size - 1)]
    down = [(j, i) for i, j in up]
    before = lax.ppermute(jnp.stack([geopotential[-EDGE:], meridional[-EDGE:]]), "tm", up)
    after = lax.ppermute(jnp.stack([geopotential[:EDGE], meridional[:EDGE]]), "tm", down)
    halo = jnp.concatenate([before, after], axis=1)

    counts = jnp.sum((jnp.arange(DAYS)[:, None] == day_index[None, :]).astype(F32), axis=1)
    counts = lax.psum(counts, "tm")
    gap = jnp.abs(jnp.arange(DROWS)[:, None] - jnp.arange(DAYS)[None, :])
    near = (gap <= WIN) | (gap >= DAYS - WIN)
    tallies = jnp.sum(jnp.where(near, counts[None, :], 0.0), axis=1)
    tally = jnp.broadcast_to(jnp.where(jnp.arange(DROWS) < DAYS, tallies, 1.0)[:, None], (DROWS, LAT))

    dma = pltpu.SemaphoreType.DMA
    mean = pl.pallas_call(
        functools.partial(mean_kernel, n, rows_f, float(lon_total)),
        out_shape=jax.ShapeDtypeStruct((2 * rows_f, LAT), F32),
        in_specs=[vmem()] * 3,
        out_specs=vmem(),
        scratch_shapes=[
            pltpu.VMEM((2 * rows_f, LAT), BF16),
            pltpu.VMEM((n - 1, share, LAT), BF16),
            dma((n - 1,)), dma((n - 1,)), dma((n - 1,)), dma((n - 1,)),
        ],
        compiler_params=pltpu.CompilerParams(collective_id=0, has_side_effects=True, vmem_limit_bytes=LIMIT),
    )(geopotential, meridional, halo)

    raw = pl.pallas_call(
        functools.partial(day_kernel, rows_f),
        out_shape=jax.ShapeDtypeStruct((3 * DROWS, width), F32),
        in_specs=[vmem()] * 6,
        out_specs=vmem(),
        scratch_shapes=[
            pltpu.VMEM((frames + 2 * EDGE, 2 * width), BF16),
            pltpu.VMEM((frames, 3 * width), BF16),
            pltpu.VMEM((DROWS, frames), BF16),
        ],
        compiler_params=pltpu.CompilerParams(vmem_limit_bytes=LIMIT),
    )(geopotential, meridional, halo, mean, day_index.reshape(1, frames), taps_matrix())

    quarter = 3 * DROWS // 4
    zshare = -(-quarter // (8 * n)) * 8
    zrows = n * zshare
    climate, zonal = pl.pallas_call(
        functools.partial(climate_kernel, n, zrows, float(lon_total)),
        out_shape=(
            jax.ShapeDtypeStruct((3 * DROWS, width), F32),
            jax.ShapeDtypeStruct((4, zrows, LAT), F32),
        ),
        in_specs=[vmem()] * 2,
        out_specs=(vmem(), vmem()),
        scratch_shapes=[
            pltpu.VMEM((3 * DROWS, width // 2), F32),
            pltpu.VMEM((3 * DROWS, width // 2), BF16),
            pltpu.VMEM((3 * DROWS, width // 2), BF16),
            pltpu.VMEM((zrows, LAT), F32),
            pltpu.VMEM((n - 1, zshare, LAT), F32),
            dma((6,)),
            dma((n - 1,)), dma((n - 1,)), dma((n - 1,)), dma((n - 1,)),
            dma((3,)), dma((3,)),
        ],
        compiler_params=pltpu.CompilerParams(collective_id=1, has_side_effects=True, vmem_limit_bytes=LIMIT),
    )(raw, tally)
    climate = climate.reshape(3, DROWS, width)[:, :DAYS]
    zonal = zonal[:, :quarter].reshape(3, DROWS, LAT)[:, :DAYS]
    return (climate, zonal)


def solution(mesh):
    return jax.shard_map(
        local,
        mesh=mesh,
        in_specs=(P("tm", "cells"), P("tm", "cells"), P("tm")),
        out_specs=(P(None, None, "cells"), P()),
        check_vma=False,
    )
```

```python
import functools

import jax
import jax.numpy as jnp
import numpy as np
from jax import lax
from jax.experimental import pallas as pl
from jax.experimental.pallas import tpu as pltpu
from jax.sharding import PartitionSpec as P

LAT = 128
HALF = 15
WIN = 7
DAYS = 365
DROWS = 384
EDGE = 16
TILE = 128
SLAB = TILE + 2 * EDGE
LIMIT = 48 * 1024 * 1024
MESH = pl.DeviceIdType.MESH
F32 = jnp.float32
BF16 = jnp.bfloat16


def vmem():
    return pl.BlockSpec(memory_space=pltpu.VMEM)


def taps_matrix():
    k = np.arange(SLAB)[None, :] - np.arange(TILE)[:, None] - EDGE
    x = np.where(k == 0, 1.0, k).astype(np.float64)
    response = (np.sin(np.pi * x) - np.sin(0.25 * np.pi * x)) / (np.pi * x)
    smoother = np.sin(np.pi * x / (HALF + 1)) / (np.pi * x / (HALF + 1))
    w = np.where(k == 0, 0.75, response * smoother)
    return jnp.asarray(np.where(np.abs(k) <= HALF, w, 0.0).astype(np.float32)).astype(BF16)


def lane_sum(block):
    total = block[:, :LAT].astype(F32)
    for start in range(LAT, block.shape[1], LAT):
        total = total + block[:, start : start + LAT].astype(F32)
    return total


def mean_kernel(
    n, rows_f, lon_total, geo, mer, mean, halo, part, inbox, hsem, ssem, rsem, gssem, grsem, fssem, frsem
):
    me = lax.axis_index("cells")
    tm = lax.axis_index("tm")
    lo = lax.rem(me, 2)
    partner = me + 1 - 2 * lo
    frames = geo.shape[0]
    share = part.shape[0] // n
    right, left = lax.rem(tm + 1, 4), lax.rem(tm + 3, 4)
    barrier = pltpu.get_barrier_semaphore()
    for k in range(1, n):
        pl.semaphore_signal(barrier, inc=1, device_id={"cells": lax.rem(me + k, n)}, device_id_type=MESH)
    for peer in (right, left):
        pl.semaphore_signal(barrier, inc=1, device_id={"tm": peer}, device_id_type=MESH)
    pl.semaphore_wait(barrier, n + 1)

    edges = []
    for f, ref in enumerate((geo, mer)):
        for side, (peer, start) in enumerate(((right, frames - EDGE), (left, 0))):
            slot = 2 * f + side
            copy = pltpu.make_async_remote_copy(
                src_ref=ref.at[start : start + EDGE],
                dst_ref=halo.at[f, side * EDGE : (side + 1) * EDGE],
                send_sem=hsem.at[slot],
                recv_sem=hsem.at[4 + slot],
                device_id={"tm": peer},
                device_id_type=MESH,
            )
            copy.start()
            edges.append(copy)

    for f, ref in enumerate((geo, mer)):

        @pl.loop(0, frames // 256)
        def _(i):
            r = pl.multiple_of(i * 256, 256)
            part[pl.ds(f * rows_f + r, 256), :] = lane_sum(ref[pl.ds(r, 256), :]).astype(BF16)

    for copy in edges:
        copy.wait()
    for f in range(2):
        base = f * rows_f + frames
        for side, inner in enumerate((tm > 0, tm < 3)):
            keep = jnp.where(inner, 1.0, 0.0).astype(F32)
            dst = slice(side * EDGE, (side + 1) * EDGE)
            halo[f, dst] = (halo[f, dst].astype(F32) * keep).astype(BF16)
        part[base : base + 2 * EDGE, :] = lane_sum(halo[f]).astype(BF16)
        rest = rows_f - frames - 2 * EDGE
        if rest:
            part[base + 2 * EDGE : base + 2 * EDGE + rest, :] = jnp.zeros((rest, LAT), BF16)

    copies = []
    for k in range(1, n):
        peer = lax.rem(me + k, n)
        copy = pltpu.make_async_remote_copy(
            src_ref=part.at[pl.ds(pl.multiple_of(peer * share, 16), share)],
            dst_ref=inbox.at[k - 1],
            send_sem=ssem.at[k - 1],
            recv_sem=rsem.at[k - 1],
            device_id={"cells": peer},
            device_id_type=MESH,
        )
        copy.start()
        copies.append(copy)
    mine = pl.ds(pl.multiple_of(me * share, 16), share)
    total = part[mine, :].astype(F32)
    for k in range(1, n):
        copies[k - 1].wait_recv()
        total = total + inbox[k - 1].astype(F32)
    mean[mine, :] = total / lon_total

    def spread(source, peer, send_sem, recv_sem):
        rows = mean.at[pl.ds(pl.multiple_of(source * share, 16), share)]
        return pltpu.make_async_remote_copy(
            src_ref=rows, dst_ref=rows, send_sem=send_sem, recv_sem=recv_sem,
            device_id={"cells": peer}, device_id_type=MESH,
        )

    m = n // 2
    passes = [spread(me, partner, fssem.at[0], frsem.at[0])]
    passes[0].start()
    gathers = []
    for k in range(1, m):
        copy = spread(me, lax.rem(me + 2 * k, n), gssem.at[k - 1], grsem.at[k - 1])
        copy.start()
        gathers.append(copy)
    for k in range(1, m):
        source = lax.rem(me + n - 2 * k, n)
        spread(source, source, gssem.at[k - 1], grsem.at[k - 1]).wait_recv()
        copy = spread(source, partner, fssem.at[k], frsem.at[k])
        copy.start()
        passes.append(copy)
    for k in range(m):
        source = lax.rem(partner + n - 2 * k, n)
        spread(source, partner, fssem.at[k], frsem.at[k]).wait_recv()
    for copy in copies + gathers + passes:
        copy.wait_send()


def day_kernel(rows_f, geo, mer, halo, mean, days, taps, raw, counts, padded, products, onehot):
    frames, width = geo.shape
    lons = width // LAT

    def put(field, dst, block, m):
        for j in range(lons):
            cols = slice(field * width + j * LAT, field * width + (j + 1) * LAT)
            padded[dst, cols] = (block[:, j * LAT : (j + 1) * LAT].astype(F32) - m).astype(BF16)

    for f, ref in enumerate((geo, mer)):
        base = f * rows_f + frames
        put(f, slice(0, EDGE), halo[f, :EDGE], mean[base : base + EDGE, :])
        put(f, slice(frames + EDGE, frames + 2 * EDGE), halo[f, EDGE:], mean[base + EDGE : base + 2 * EDGE, :])

        @pl.loop(0, frames // 128)
        def _(i):
            r = pl.multiple_of(i * 128, 128)
            put(f, pl.ds(r + EDGE, 128), ref[pl.ds(r, 128), :], mean[pl.ds(f * rows_f + r, 128), :])

    @pl.loop(0, frames // TILE)
    def _(i):
        r = pl.multiple_of(i * TILE, TILE)
        hit = lax.broadcasted_iota(jnp.int32, (DROWS, TILE), 0) == days[:, pl.ds(r, TILE)]
        onehot[:, pl.ds(r, TILE)] = jnp.where(hit, 1.0, 0.0).astype(BF16)
        for j in range(width // 256):
            lo, hi = j * 256, (j + 1) * 256
            a = jnp.dot(taps[...], padded[pl.ds(r, SLAB), lo:hi], preferred_element_type=F32)
            b = jnp.dot(taps[...], padded[pl.ds(r, SLAB), width + lo : width + hi], preferred_element_type=F32)
            products[pl.ds(r, TILE), lo:hi] = (a * a).astype(BF16)
            products[pl.ds(r, TILE), width + lo : width + hi] = (b * b).astype(BF16)
            products[pl.ds(r, TILE), 2 * width + lo : 2 * width + hi] = (a * b).astype(BF16)

    counts[...] = lax.dot_general(
        jnp.ones((8, frames), BF16), onehot[...], (((1,), (1,)), ((), ())), preferred_element_type=F32
    )
    for s in range(3):

        @pl.loop(0, width // 256)
        def _(j):
            c = pl.multiple_of(j * 256, 256)
            raw[s * DROWS : (s + 1) * DROWS, pl.ds(c, 256)] = jnp.dot(
                onehot[...], products[:, pl.ds(s * width + c, 256)], preferred_element_type=F32
            )


def climate_kernel(
    n, zrows, lon_total, raw, counts, climate, zonal, inbox, own, other, cbox, zhalf, zother, zpart, zbox,
    fsem, ssem, tsem, csem, xsem, zsend, zrecv, gsend, grecv, tsend, trecv,
):
    me = lax.axis_index("cells")
    tm = lax.axis_index("tm")
    core = lax.rem(tm, 2)
    partner = tm + 1 - 2 * core
    across = lax.rem(tm + 2, 4)
    half = raw.shape[1] // 2
    share = zrows // n
    barrier = pltpu.get_barrier_semaphore()
    for k in range(1, n):
        pl.semaphore_signal(barrier, inc=1, device_id={"cells": lax.rem(me + k, n)}, device_id_type=MESH)
    for k in range(1, 4):
        pl.semaphore_signal(barrier, inc=1, device_id={"tm": lax.rem(tm + k, 4)}, device_id_type=MESH)
    pl.semaphore_wait(barrier, n + 2)

    mine = pl.ds(pl.multiple_of(core * half, 128), half)
    theirs = pl.ds(pl.multiple_of((1 - core) * half, 128), half)
    parts = [slice(s * DROWS, (s + 1) * DROWS) for s in range(3)]
    first, second, third, tell = [], [], [], []
    for s, rows in enumerate(parts):
        first.append(pltpu.make_async_remote_copy(
            src_ref=raw.at[rows, theirs], dst_ref=inbox.at[rows], send_sem=fsem.at[s], recv_sem=fsem.at[3 + s],
            device_id={"tm": partner}, device_id_type=MESH,
        ))
        first[s].start()
    for k in range(1, 4):
        tell.append(pltpu.make_async_remote_copy(
            src_ref=counts, dst_ref=cbox.at[k - 1], send_sem=csem.at[k - 1], recv_sem=csem.at[2 + k],
            device_id={"tm": lax.rem(tm + k, 4)}, device_id_type=MESH,
        ))
        tell[-1].start()
    d = lax.broadcasted_iota(jnp.int32, (DROWS, DROWS), 0)
    e = lax.broadcasted_iota(jnp.int32, (DROWS, DROWS), 1)
    gap = jnp.abs(d - e)
    inside = jnp.where(((gap <= WIN) | (gap >= DAYS - WIN)) & (e < DAYS), 1.0, 0.0).astype(F32)
    window = inside.astype(BF16)
    for s, rows in enumerate(parts):
        first[s].wait_recv()
        own[rows, :] = (raw[rows, mine] + inbox[rows, :]).astype(BF16)
        second.append(pltpu.make_async_remote_copy(
            src_ref=own.at[rows], dst_ref=other.at[rows], send_sem=ssem.at[s], recv_sem=ssem.at[3 + s],
            device_id={"tm": across}, device_id_type=MESH,
        ))
        second[s].start()
    for rows in parts:
        inbox[rows, :] = jnp.dot(window, own[rows, :], preferred_element_type=F32)
    row = counts[0:1, :]
    for k in range(3):
        tell[k].wait()
        row = row + cbox[k, 0:1, :]
    tally = jnp.broadcast_to(jnp.sum(inside * row, axis=1, keepdims=True), (DROWS, LAT))
    for s, rows in enumerate(parts):
        second[s].wait_recv()
        total = inbox[rows, :] + jnp.dot(window, other[rows, :], preferred_element_type=F32)
        zonal_sum = jnp.zeros((DROWS, LAT), F32)
        for j in range(half // LAT):
            cols = pl.ds(pl.multiple_of(core * half + j * LAT, 128), LAT)
            value = total[:, j * LAT : (j + 1) * LAT] / tally
            climate[rows, cols] = value
            zonal_sum = zonal_sum + value
        zhalf[rows, :] = zonal_sum
        third.append(pltpu.make_async_remote_copy(
            src_ref=climate.at[rows, mine], dst_ref=climate.at[rows, mine], send_sem=tsem.at[s],
            recv_sem=tsem.at[3 + s], device_id={"tm": partner}, device_id_type=MESH,
        ))
        if s < 2:
            third[s].start()

    quarter = climate.shape[0] // 4
    swap = pltpu.make_async_remote_copy(
        src_ref=zhalf.at[pl.ds(pl.multiple_of(partner * quarter, 8), quarter)], dst_ref=zother,
        send_sem=xsem.at[0], recv_sem=xsem.at[1], device_id={"tm": partner}, device_id_type=MESH,
    )
    swap.start()
    third[2].start()
    if zrows > quarter:
        zpart[quarter:, :] = jnp.zeros((zrows - quarter, LAT), F32)
    swap.wait()
    zpart[:quarter, :] = zhalf[pl.ds(pl.multiple_of(tm * quarter, 8), quarter), :] + zother[...]
    copies = []
    for k in range(1, n):
        peer = lax.rem(me + k, n)
        copy = pltpu.make_async_remote_copy(
            src_ref=zpart.at[pl.ds(pl.multiple_of(peer * share, 8), share)],
            dst_ref=zbox.at[k - 1], send_sem=zsend.at[k - 1], recv_sem=zrecv.at[k - 1],
            device_id={"cells": peer}, device_id_type=MESH,
        )
        copy.start()
        copies.append(copy)
    block = pl.ds(pl.multiple_of(me * share, 8), share)
    total = zpart[block, :]
    for k in range(1, n):
        copies[k - 1].wait_recv()
        total = total + zbox[k - 1]
    zonal[tm, block, :] = total / lon_total
    gathers = []
    for k in range(1, n):
        copy = pltpu.make_async_remote_copy(
            src_ref=zonal.at[tm, block], dst_ref=zonal.at[tm, block],
            send_sem=gsend.at[k - 1], recv_sem=grecv.at[k - 1],
            device_id={"cells": lax.rem(me + k, n)}, device_id_type=MESH,
        )
        copy.start()
        gathers.append(copy)
    for k in range(1, n):
        copies[k - 1].wait_send()
        gathers[k - 1].wait_send()
        source = lax.rem(me + n - k, n)
        there = zonal.at[tm, pl.ds(pl.multiple_of(source * share, 8), share)]
        pltpu.make_async_remote_copy(
            src_ref=there, dst_ref=there, send_sem=gsend.at[k - 1], recv_sem=grecv.at[k - 1],
            device_id={"cells": source}, device_id_type=MESH,
        ).wait_recv()
    spreads = []
    for k in range(1, 4):
        copy = pltpu.make_async_remote_copy(
            src_ref=zonal.at[tm], dst_ref=zonal.at[tm],
            send_sem=tsend.at[k - 1], recv_sem=trecv.at[k - 1],
            device_id={"tm": lax.rem(tm + k, 4)}, device_id_type=MESH,
        )
        copy.start()
        spreads.append(copy)
    for k in range(1, 4):
        spreads[k - 1].wait_send()
        source = lax.rem(tm + 4 - k, 4)
        pltpu.make_async_remote_copy(
            src_ref=zonal.at[source], dst_ref=zonal.at[source],
            send_sem=tsend.at[k - 1], recv_sem=trecv.at[k - 1],
            device_id={"tm": source}, device_id_type=MESH,
        ).wait_recv()
    for s, rows in enumerate(parts):
        first[s].wait_send()
        second[s].wait_send()
        third[s].wait_send()
        pltpu.make_async_remote_copy(
            src_ref=climate.at[rows, theirs], dst_ref=climate.at[rows, theirs], send_sem=tsem.at[s],
            recv_sem=tsem.at[3 + s], device_id={"tm": partner}, device_id_type=MESH,
        ).wait_recv()


def local(geopotential, meridional, day_index):
    frames, width = geopotential.shape
    n = lax.axis_size("cells")
    lon_total = width // LAT * n
    step = 8 * n
    rows_f = -(-(frames + 2 * EDGE) // step) * step
    share = 2 * rows_f // n

    dma = pltpu.SemaphoreType.DMA
    mean, halo = pl.pallas_call(
        functools.partial(mean_kernel, n, rows_f, float(lon_total)),
        out_shape=(
            jax.ShapeDtypeStruct((2 * rows_f, LAT), F32),
            jax.ShapeDtypeStruct((2, 2 * EDGE, width), BF16),
        ),
        in_specs=[vmem()] * 2,
        out_specs=(vmem(), vmem()),
        scratch_shapes=[
            pltpu.VMEM((2 * rows_f, LAT), BF16),
            pltpu.VMEM((n - 1, share, LAT), BF16),
            dma((8,)), dma((n - 1,)), dma((n - 1,)),
            dma((n // 2 - 1,)), dma((n // 2 - 1,)), dma((n // 2,)), dma((n // 2,)),
        ],
        compiler_params=pltpu.CompilerParams(collective_id=0, has_side_effects=True, vmem_limit_bytes=LIMIT),
    )(geopotential, meridional)

    raw, counts = pl.pallas_call(
        functools.partial(day_kernel, rows_f),
        out_shape=(
            jax.ShapeDtypeStruct((3 * DROWS, width), F32),
            jax.ShapeDtypeStruct((8, DROWS), F32),
        ),
        in_specs=[vmem()] * 6,
        out_specs=(vmem(), vmem()),
        scratch_shapes=[
            pltpu.VMEM((frames + 2 * EDGE, 2 * width), BF16),
            pltpu.VMEM((frames, 3 * width), BF16),
            pltpu.VMEM((DROWS, frames), BF16),
        ],
        compiler_params=pltpu.CompilerParams(vmem_limit_bytes=LIMIT),
    )(geopotential, meridional, halo, mean, day_index.reshape(1, frames), taps_matrix())

    quarter = 3 * DROWS // 4
    zshare = -(-quarter // (8 * n)) * 8
    zrows = n * zshare
    climate, zonal = pl.pallas_call(
        functools.partial(climate_kernel, n, zrows, float(lon_total)),
        out_shape=(
            jax.ShapeDtypeStruct((3 * DROWS, width), F32),
            jax.ShapeDtypeStruct((4, zrows, LAT), F32),
        ),
        in_specs=[vmem()] * 2,
        out_specs=(vmem(), vmem()),
        scratch_shapes=[
            pltpu.VMEM((3 * DROWS, width // 2), F32),
            pltpu.VMEM((3 * DROWS, width // 2), BF16),
            pltpu.VMEM((3 * DROWS, width // 2), BF16),
            pltpu.VMEM((3, 8, DROWS), F32),
            pltpu.VMEM((3 * DROWS, LAT), F32),
            pltpu.VMEM((quarter, LAT), F32),
            pltpu.VMEM((zrows, LAT), F32),
            pltpu.VMEM((n - 1, zshare, LAT), F32),
            dma((6,)), dma((6,)), dma((6,)), dma((6,)), dma((2,)),
            dma((n - 1,)), dma((n - 1,)), dma((n - 1,)), dma((n - 1,)),
            dma((3,)), dma((3,)),
        ],
        compiler_params=pltpu.CompilerParams(collective_id=1, has_side_effects=True, vmem_limit_bytes=LIMIT),
    )(raw, counts)
    climate = climate.reshape(3, DROWS, width)[:, :DAYS]
    zonal = zonal[:, :quarter].reshape(3, DROWS, LAT)[:, :DAYS]
    return (climate, zonal)


def solution(mesh):
    return jax.shard_map(
        local,
        mesh=mesh,
        in_specs=(P("tm", "cells"), P("tm", "cells"), P("tm")),
        out_specs=(P(None, None, "cells"), P()),
        check_vma=False,
    )
```

```python
import functools

import jax
import jax.numpy as jnp
import numpy as np
from jax import lax
from jax.experimental import pallas as pl
from jax.experimental.pallas import tpu as pltpu
from jax.sharding import PartitionSpec as P

LAT = 128
HALF = 15
WIN = 7
DAYS = 365
DROWS = 384
EDGE = 16
TILE = 128
SLAB = TILE + 2 * EDGE
LIMIT = 48 * 1024 * 1024
MESH = pl.DeviceIdType.MESH
F32 = jnp.float32
BF16 = jnp.bfloat16


def vmem():
    return pl.BlockSpec(memory_space=pltpu.VMEM)


def taps_matrix():
    k = np.arange(SLAB)[None, :] - np.arange(TILE)[:, None] - EDGE
    x = np.where(k == 0, 1.0, k).astype(np.float64)
    response = (np.sin(np.pi * x) - np.sin(0.25 * np.pi * x)) / (np.pi * x)
    smoother = np.sin(np.pi * x / (HALF + 1)) / (np.pi * x / (HALF + 1))
    w = np.where(k == 0, 0.75, response * smoother)
    return jnp.asarray(np.where(np.abs(k) <= HALF, w, 0.0).astype(np.float32)).astype(BF16)


def lane_sum(block):
    total = block[:, :LAT].astype(F32)
    for start in range(LAT, block.shape[1], LAT):
        total = total + block[:, start : start + LAT].astype(F32)
    return total


def eddy_kernel(
    n, lon_total, zrows, pieces, geo_in, mer_in, days, taps, climate, zonal,
    geo, mer, halo, part, mbox, mean, padded, products, onehot, counts, give, keep,
    inbox, own, other, cbox, zhalf, zother, zpart, zbox,
    lsem, hsem, rsend, rrecv, gssem, grsem, fssem, frsem,
    fsem, ssem, tsem, csem, xsem, zsend, zrecv, gsend, grecv, tsend, trecv,
):
    me = lax.axis_index("cells")
    tm = lax.axis_index("tm")
    lo = lax.rem(me, 2)
    mate = me + 1 - 2 * lo
    core = lax.rem(tm, 2)
    partner = tm + 1 - 2 * core
    across = lax.rem(tm + 2, 4)
    frames, width = geo.shape
    lons = width // LAT
    half = width // 2
    count = len(pieces)
    length = frames // count
    share = zrows // n
    m = n // 2
    barrier = pltpu.get_barrier_semaphore()
    for k in range(1, n):
        pl.semaphore_signal(barrier, inc=1, device_id={"cells": lax.rem(me + k, n)}, device_id_type=MESH)
    for k in range(1, 4):
        pl.semaphore_signal(barrier, inc=1, device_id={"tm": lax.rem(tm + k, 4)}, device_id_type=MESH)

    loads = []
    for p in range(count):
        rows = slice(p * length, (p + 1) * length)
        for f, (src, dst) in enumerate(((geo_in, geo), (mer_in, mer))):
            copy = pltpu.make_async_copy(src.at[rows], dst.at[rows], lsem.at[2 * p + f])
            copy.start()
            loads.append(copy)
    pl.semaphore_wait(barrier, n + 2)

    edges = []
    right, left = lax.rem(tm + 1, 4), lax.rem(tm + 3, 4)
    for f, ref in enumerate((geo_in, mer_in)):
        for side, (peer, start) in enumerate(((right, frames - EDGE), (left, 0))):
            slot = 2 * f + side
            copy = pltpu.make_async_remote_copy(
                src_ref=ref.at[start : start + EDGE],
                dst_ref=halo.at[f, side * EDGE : (side + 1) * EDGE],
                send_sem=hsem.at[slot],
                recv_sem=hsem.at[4 + slot],
                device_id={"tm": peer},
                device_id_type=MESH,
            )
            copy.start()
            edges.append(copy)

    sends = []
    scattered = [[] for _ in range(count)]

    def lanes(p):
        base, total_rows = pieces[p]
        loads[2 * p].wait()
        loads[2 * p + 1].wait()
        for f, ref in enumerate((geo, mer)):

            @pl.loop(0, length // 128)
            def _(i):
                r = pl.multiple_of(i * 128, 128)
                part[pl.ds(base + f * length + r, 128), :] = lane_sum(ref[pl.ds(p * length + r, 128), :]).astype(BF16)

        used = 2 * length
        if p == 0:
            for copy in edges:
                copy.wait()
            for f in range(2):
                for side, inner in enumerate((tm > 0, tm < 3)):
                    hold = jnp.where(inner, 1.0, 0.0).astype(F32)
                    dst = slice(side * EDGE, (side + 1) * EDGE)
                    halo[f, dst] = (halo[f, dst].astype(F32) * hold).astype(BF16)
                part[base + used : base + used + 2 * EDGE, :] = lane_sum(halo[f]).astype(BF16)
                used += 2 * EDGE
        if total_rows > used:
            part[base + used : base + total_rows, :] = jnp.zeros((total_rows - used, LAT), BF16)

    def chunk(p, source):
        base, total_rows = pieces[p]
        size = total_rows // n
        return pl.ds(pl.multiple_of(base + source * size, 16), size)

    def scatter(p):
        size = pieces[p][1] // n
        for k in range(1, n):
            peer = lax.rem(me + k, n)
            copy = pltpu.make_async_remote_copy(
                src_ref=part.at[chunk(p, peer)],
                dst_ref=mbox.at[p, k - 1, :size],
                send_sem=rsend.at[p, k - 1],
                recv_sem=rrecv.at[p, k - 1],
                device_id={"cells": peer},
                device_id_type=MESH,
            )
            copy.start()
            scattered[p].append(copy)
            sends.append(copy)

    def spread(p, source, peer, send_sem, recv_sem):
        rows = mean.at[chunk(p, source)]
        return pltpu.make_async_remote_copy(
            src_ref=rows, dst_ref=rows, send_sem=send_sem, recv_sem=recv_sem,
            device_id={"cells": peer}, device_id_type=MESH,
        )

    def reduce(p):
        size = pieces[p][1] // n
        mine = chunk(p, me)
        total = part[mine, :].astype(F32)
        for k in range(1, n):
            scattered[p][k - 1].wait_recv()
            total = total + mbox[p, k - 1, :size].astype(F32)
        mean[mine, :] = total / lon_total
        copy = spread(p, me, mate, fssem.at[p, 0], frsem.at[p, 0])
        copy.start()
        sends.append(copy)
        for k in range(1, m):
            copy = spread(p, me, lax.rem(me + 2 * k, n), gssem.at[p, k - 1], grsem.at[p, k - 1])
            copy.start()
            sends.append(copy)

    def forward(p):
        for k in range(1, m):
            source = lax.rem(me + n - 2 * k, n)
            spread(p, source, source, gssem.at[p, k - 1], grsem.at[p, k - 1]).wait_recv()
            copy = spread(p, source, mate, fssem.at[p, k], frsem.at[p, k])
            copy.start()
            sends.append(copy)

    def settle(p):
        for k in range(m):
            source = lax.rem(mate + n - 2 * k, n)
            spread(p, source, mate, fssem.at[p, k], frsem.at[p, k]).wait_recv()

    def put(field, dst, block, value):
        for j in range(lons):
            cols = slice(field * width + j * LAT, field * width + (j + 1) * LAT)
            padded[dst, cols] = (block[:, j * LAT : (j + 1) * LAT].astype(F32) - value).astype(BF16)

    def anomalies(p):
        base = pieces[p][0]
        for f, ref in enumerate((geo, mer)):
            if p == 0:
                at = base + 2 * length + f * 2 * EDGE
                put(f, slice(0, EDGE), halo[f, :EDGE], mean[at : at + EDGE, :])
                end = frames + EDGE
                put(f, slice(end, end + EDGE), halo[f, EDGE:], mean[at + EDGE : at + 2 * EDGE, :])

            @pl.loop(0, length // 128)
            def _(i):
                r = pl.multiple_of(i * 128, 128)
                dst = pl.ds(pl.multiple_of(p * length + EDGE + r, 16), 128)
                put(f, dst, ref[pl.ds(p * length + r, 128), :], mean[pl.ds(base + f * length + r, 128), :])

    def filtering(p):
        tiles = length // TILE
        start = p * tiles - 1 if p else 0
        stop = (p + 1) * tiles - (0 if p == count - 1 else 1)

        @pl.loop(start, stop)
        def _(i):
            r = pl.multiple_of(i * TILE, TILE)
            for j in range(width // 256):
                a0, a1 = j * 256, (j + 1) * 256
                a = jnp.dot(taps[...], padded[pl.ds(r, SLAB), a0:a1], preferred_element_type=F32)
                b = jnp.dot(taps[...], padded[pl.ds(r, SLAB), width + a0 : width + a1], preferred_element_type=F32)
                products[pl.ds(r, TILE), a0:a1] = (a * a).astype(BF16)
                products[pl.ds(r, TILE), width + a0 : width + a1] = (b * b).astype(BF16)
                products[pl.ds(r, TILE), 2 * width + a0 : 2 * width + a1] = (a * b).astype(BF16)

    tell = []
    for t in range(count + 3):
        if t < count:
            lanes(t)
            scatter(t)
        if 1 <= t <= count:
            if t == 1:

                @pl.loop(0, frames // TILE)
                def _(i):
                    r = pl.multiple_of(i * TILE, TILE)
                    hit = lax.broadcasted_iota(jnp.int32, (DROWS, TILE), 0) == days[:, pl.ds(r, TILE)]
                    onehot[:, pl.ds(r, TILE)] = jnp.where(hit, 1.0, 0.0).astype(BF16)

                counts[...] = lax.dot_general(
                    jnp.ones((8, frames), BF16), onehot[...], (((1,), (1,)), ((), ())), preferred_element_type=F32
                )
                for k in range(1, 4):
                    copy = pltpu.make_async_remote_copy(
                        src_ref=counts, dst_ref=cbox.at[k - 1], send_sem=csem.at[k - 1], recv_sem=csem.at[2 + k],
                        device_id={"tm": lax.rem(tm + k, 4)}, device_id_type=MESH,
                    )
                    copy.start()
                    tell.append(copy)
            reduce(t - 1)
        if 2 <= t <= count + 1:
            forward(t - 2)
        if t >= 3:
            settle(t - 3)
            anomalies(t - 3)
            filtering(t - 3)

    mine = pl.ds(pl.multiple_of(core * half, 128), half)
    theirs = pl.ds(pl.multiple_of((1 - core) * half, 128), half)
    parts = [slice(s * DROWS, (s + 1) * DROWS) for s in range(3)]
    first, second, third = [], [], []
    for s, rows in enumerate(parts):
        cols = pl.ds(pl.multiple_of(s * width + (1 - core) * half, 128), half)
        give[rows, :] = jnp.dot(onehot[...], products[:, cols], preferred_element_type=F32)
        first.append(pltpu.make_async_remote_copy(
            src_ref=give.at[rows], dst_ref=inbox.at[rows], send_sem=fsem.at[s], recv_sem=fsem.at[3 + s],
            device_id={"tm": partner}, device_id_type=MESH,
        ))
        first[s].start()
    for s, rows in enumerate(parts):
        cols = pl.ds(pl.multiple_of(s * width + core * half, 128), half)
        keep[rows, :] = jnp.dot(onehot[...], products[:, cols], preferred_element_type=F32)
        first[s].wait_recv()
        own[rows, :] = (keep[rows, :] + inbox[rows, :]).astype(BF16)
        second.append(pltpu.make_async_remote_copy(
            src_ref=own.at[rows], dst_ref=other.at[rows], send_sem=ssem.at[s], recv_sem=ssem.at[3 + s],
            device_id={"tm": across}, device_id_type=MESH,
        ))
        second[s].start()
    d = lax.broadcasted_iota(jnp.int32, (DROWS, DROWS), 0)
    e = lax.broadcasted_iota(jnp.int32, (DROWS, DROWS), 1)
    gap = jnp.abs(d - e)
    inside = jnp.where(((gap <= WIN) | (gap >= DAYS - WIN)) & (e < DAYS), 1.0, 0.0).astype(F32)
    window = inside.astype(BF16)
    for rows in parts:
        inbox[rows, :] = jnp.dot(window, own[rows, :], preferred_element_type=F32)
    row = counts[0:1, :]
    for k in range(3):
        tell[k].wait()
        row = row + cbox[k, 0:1, :]
    tally = jnp.broadcast_to(jnp.sum(inside * row, axis=1, keepdims=True), (DROWS, LAT))
    for s, rows in enumerate(parts):
        second[s].wait_recv()
        total = inbox[rows, :] + jnp.dot(window, other[rows, :], preferred_element_type=F32)
        zonal_sum = jnp.zeros((DROWS, LAT), F32)
        for j in range(half // LAT):
            cols = pl.ds(pl.multiple_of(core * half + j * LAT, 128), LAT)
            value = total[:, j * LAT : (j + 1) * LAT] / tally
            climate[rows, cols] = value
            zonal_sum = zonal_sum + value
        zhalf[rows, :] = zonal_sum
        third.append(pltpu.make_async_remote_copy(
            src_ref=climate.at[rows, mine], dst_ref=climate.at[rows, mine], send_sem=tsem.at[s],
            recv_sem=tsem.at[3 + s], device_id={"tm": partner}, device_id_type=MESH,
        ))
        if s < 2:
            third[s].start()

    quarter = climate.shape[0] // 4
    swap = pltpu.make_async_remote_copy(
        src_ref=zhalf.at[pl.ds(pl.multiple_of(partner * quarter, 8), quarter)], dst_ref=zother,
        send_sem=xsem.at[0], recv_sem=xsem.at[1], device_id={"tm": partner}, device_id_type=MESH,
    )
    swap.start()
    third[2].start()
    if zrows > quarter:
        zpart[quarter:, :] = jnp.zeros((zrows - quarter, LAT), F32)
    swap.wait()
    zpart[:quarter, :] = zhalf[pl.ds(pl.multiple_of(tm * quarter, 8), quarter), :] + zother[...]
    copies = []
    for k in range(1, n):
        peer = lax.rem(me + k, n)
        copy = pltpu.make_async_remote_copy(
            src_ref=zpart.at[pl.ds(pl.multiple_of(peer * share, 8), share)],
            dst_ref=zbox.at[k - 1], send_sem=zsend.at[k - 1], recv_sem=zrecv.at[k - 1],
            device_id={"cells": peer}, device_id_type=MESH,
        )
        copy.start()
        copies.append(copy)
    block = pl.ds(pl.multiple_of(me * share, 8), share)
    total = zpart[block, :]
    for k in range(1, n):
        copies[k - 1].wait_recv()
        total = total + zbox[k - 1]
    zonal[tm, block, :] = total / lon_total
    gathers = []
    for k in range(1, n):
        copy = pltpu.make_async_remote_copy(
            src_ref=zonal.at[tm, block], dst_ref=zonal.at[tm, block],
            send_sem=gsend.at[k - 1], recv_sem=grecv.at[k - 1],
            device_id={"cells": lax.rem(me + k, n)}, device_id_type=MESH,
        )
        copy.start()
        gathers.append(copy)
    for k in range(1, n):
        copies[k - 1].wait_send()
        gathers[k - 1].wait_send()
        source = lax.rem(me + n - k, n)
        there = zonal.at[tm, pl.ds(pl.multiple_of(source * share, 8), share)]
        pltpu.make_async_remote_copy(
            src_ref=there, dst_ref=there, send_sem=gsend.at[k - 1], recv_sem=grecv.at[k - 1],
            device_id={"cells": source}, device_id_type=MESH,
        ).wait_recv()
    spreads = []
    for k in range(1, 4):
        copy = pltpu.make_async_remote_copy(
            src_ref=zonal.at[tm], dst_ref=zonal.at[tm],
            send_sem=tsend.at[k - 1], recv_sem=trecv.at[k - 1],
            device_id={"tm": lax.rem(tm + k, 4)}, device_id_type=MESH,
        )
        copy.start()
        spreads.append(copy)
    for k in range(1, 4):
        spreads[k - 1].wait_send()
        source = lax.rem(tm + 4 - k, 4)
        pltpu.make_async_remote_copy(
            src_ref=zonal.at[source], dst_ref=zonal.at[source],
            send_sem=tsend.at[k - 1], recv_sem=trecv.at[k - 1],
            device_id={"tm": source}, device_id_type=MESH,
        ).wait_recv()
    for copy in sends:
        copy.wait_send()
    for s, rows in enumerate(parts):
        first[s].wait_send()
        second[s].wait_send()
        third[s].wait_send()
        pltpu.make_async_remote_copy(
            src_ref=climate.at[rows, theirs], dst_ref=climate.at[rows, theirs], send_sem=tsem.at[s],
            recv_sem=tsem.at[3 + s], device_id={"tm": partner}, device_id_type=MESH,
        ).wait_recv()


def local(geopotential, meridional, day_index):
    frames, width = geopotential.shape
    n = lax.axis_size("cells")
    lon_total = width // LAT * n
    step = 16 * n
    count = 4
    pieces, base = [], 0
    for p in range(count):
        rows = 2 * (frames // count) + (4 * EDGE if p == 0 else 0)
        rows = -(-rows // step) * step
        pieces.append((base, rows))
        base += rows
    share = max(rows for _, rows in pieces) // n
    quarter = 3 * DROWS // 4
    zshare = -(-quarter // (8 * n)) * 8
    zrows = n * zshare
    half = width // 2

    dma = pltpu.SemaphoreType.DMA
    climate, zonal = pl.pallas_call(
        functools.partial(eddy_kernel, n, float(lon_total), zrows, pieces),
        out_shape=(
            jax.ShapeDtypeStruct((3 * DROWS, width), F32),
            jax.ShapeDtypeStruct((4, zrows, LAT), F32),
        ),
        in_specs=[pl.BlockSpec(memory_space=pl.ANY)] * 2 + [vmem()] * 2,
        out_specs=(vmem(), vmem()),
        scratch_shapes=[
            pltpu.VMEM((frames, width), BF16),
            pltpu.VMEM((frames, width), BF16),
            pltpu.VMEM((2, 2 * EDGE, width), BF16),
            pltpu.VMEM((base, LAT), BF16),
            pltpu.VMEM((count, n - 1, share, LAT), BF16),
            pltpu.VMEM((base, LAT), F32),
            pltpu.VMEM((frames + 2 * EDGE, 2 * width), BF16),
            pltpu.VMEM((frames, 3 * width), BF16),
            pltpu.VMEM((DROWS, frames), BF16),
            pltpu.VMEM((8, DROWS), F32),
            pltpu.VMEM((3 * DROWS, half), F32),
            pltpu.VMEM((3 * DROWS, half), F32),
            pltpu.VMEM((3 * DROWS, half), F32),
            pltpu.VMEM((3 * DROWS, half), BF16),
            pltpu.VMEM((3 * DROWS, half), BF16),
            pltpu.VMEM((3, 8, DROWS), F32),
            pltpu.VMEM((3 * DROWS, LAT), F32),
            pltpu.VMEM((quarter, LAT), F32),
            pltpu.VMEM((zrows, LAT), F32),
            pltpu.VMEM((n - 1, zshare, LAT), F32),
            dma((2 * count,)), dma((8,)),
            dma((count, n - 1)), dma((count, n - 1)),
            dma((count, n // 2 - 1)), dma((count, n // 2 - 1)), dma((count, n // 2)), dma((count, n // 2)),
            dma((6,)), dma((6,)), dma((6,)), dma((6,)), dma((2,)),
            dma((n - 1,)), dma((n - 1,)), dma((n - 1,)), dma((n - 1,)),
            dma((3,)), dma((3,)),
        ],
        compiler_params=pltpu.CompilerParams(collective_id=0, has_side_effects=True, vmem_limit_bytes=LIMIT),
    )(geopotential, meridional, day_index.reshape(1, frames), taps_matrix())
    climate = climate.reshape(3, DROWS, width)[:, :DAYS]
    zonal = zonal[:, :quarter].reshape(3, DROWS, LAT)[:, :DAYS]
    return (climate, zonal)


def solution(mesh):
    return jax.shard_map(
        local,
        mesh=mesh,
        in_specs=(P("tm", "cells"), P("tm", "cells"), P("tm")),
        out_specs=(P(None, None, "cells"), P()),
        check_vma=False,
    )
```

```python
import functools

import jax
import jax.numpy as jnp
import numpy as np
from jax import lax
from jax.experimental import pallas as pl
from jax.experimental.pallas import tpu as pltpu
from jax.sharding import PartitionSpec as P

LAT = 128
HALF = 15
WIN = 7
DAYS = 365
DROWS = 384
EDGE = 16
TILE = 128
SLAB = TILE + 2 * EDGE
LIMIT = 60 * 1024 * 1024
MESH = pl.DeviceIdType.MESH
F32 = jnp.float32
BF16 = jnp.bfloat16


def vmem():
    return pl.BlockSpec(memory_space=pltpu.VMEM)


def taps_matrix():
    k = np.arange(SLAB)[None, :] - np.arange(TILE)[:, None] - EDGE
    x = np.where(k == 0, 1.0, k).astype(np.float64)
    response = (np.sin(np.pi * x) - np.sin(0.25 * np.pi * x)) / (np.pi * x)
    smoother = np.sin(np.pi * x / (HALF + 1)) / (np.pi * x / (HALF + 1))
    w = np.where(k == 0, 0.75, response * smoother)
    return jnp.asarray(np.where(np.abs(k) <= HALF, w, 0.0).astype(np.float32)).astype(BF16)


def lane_sum(block):
    total = block[:, :LAT].astype(F32)
    for start in range(LAT, block.shape[1], LAT):
        total = total + block[:, start : start + LAT].astype(F32)
    return total


def eddy_kernel(
    n, lon_total, zrows, pieces, geo_in, mer_in, days, taps, climate, zonal,
    geo, mer, halo, part, mbox, mean, padded, products, onehot, counts, give, keep,
    inbox, own, other, cbox, zhalf, zother, zpart, zbox,
    lsem, hsem, rsend, rrecv, gssem, grsem, fssem, frsem,
    fsem, ssem, tsem, csem, xsem, zsend, zrecv, gsend, grecv, tsend, trecv,
):
    me = lax.axis_index("cells")
    tm = lax.axis_index("tm")
    lo = lax.rem(me, 2)
    mate = me + 1 - 2 * lo
    core = lax.rem(tm, 2)
    partner = tm + 1 - 2 * core
    across = lax.rem(tm + 2, 4)
    frames, width = geo.shape
    lons = width // LAT
    half = width // 2
    count = len(pieces)
    length = frames // count
    share = zrows // n
    m = n // 2
    barrier = pltpu.get_barrier_semaphore()
    for k in range(1, n):
        pl.semaphore_signal(barrier, inc=1, device_id={"cells": lax.rem(me + k, n)}, device_id_type=MESH)
    for k in range(1, 4):
        pl.semaphore_signal(barrier, inc=1, device_id={"tm": lax.rem(tm + k, 4)}, device_id_type=MESH)

    loads = []
    for p in range(count):
        rows = slice(p * length, (p + 1) * length)
        for f, (src, dst) in enumerate(((geo_in, geo), (mer_in, mer))):
            copy = pltpu.make_async_copy(src.at[rows], dst.at[rows], lsem.at[2 * p + f])
            copy.start()
            loads.append(copy)
    pl.semaphore_wait(barrier, n + 2)

    edges = []
    right, left = lax.rem(tm + 1, 4), lax.rem(tm + 3, 4)
    for f, ref in enumerate((geo_in, mer_in)):
        for side, (peer, start) in enumerate(((right, frames - EDGE), (left, 0))):
            slot = 2 * f + side
            copy = pltpu.make_async_remote_copy(
                src_ref=ref.at[start : start + EDGE],
                dst_ref=halo.at[f, side * EDGE : (side + 1) * EDGE],
                send_sem=hsem.at[slot],
                recv_sem=hsem.at[4 + slot],
                device_id={"tm": peer},
                device_id_type=MESH,
            )
            copy.start()
            edges.append(copy)

    sends = []
    scattered = [[] for _ in range(count)]

    def lanes(p):
        base, total_rows = pieces[p]
        loads[2 * p].wait()
        loads[2 * p + 1].wait()
        for f, ref in enumerate((geo, mer)):

            @pl.loop(0, length // 128)
            def _(i):
                r = pl.multiple_of(i * 128, 128)
                part[pl.ds(base + f * length + r, 128), :] = lane_sum(ref[pl.ds(p * length + r, 128), :]).astype(BF16)

        used = 2 * length
        if p == 0:
            for copy in edges:
                copy.wait()
            for f in range(2):
                for side, inner in enumerate((tm > 0, tm < 3)):
                    hold = jnp.where(inner, 1.0, 0.0).astype(F32)
                    dst = slice(side * EDGE, (side + 1) * EDGE)
                    halo[f, dst] = (halo[f, dst].astype(F32) * hold).astype(BF16)
                part[base + used : base + used + 2 * EDGE, :] = lane_sum(halo[f]).astype(BF16)
                used += 2 * EDGE
        if total_rows > used:
            part[base + used : base + total_rows, :] = jnp.zeros((total_rows - used, LAT), BF16)

    def chunk(p, source):
        base, total_rows = pieces[p]
        size = total_rows // n
        return pl.ds(pl.multiple_of(base + source * size, 16), size)

    def scatter(p):
        size = pieces[p][1] // n
        for k in range(1, n):
            peer = lax.rem(me + k, n)
            copy = pltpu.make_async_remote_copy(
                src_ref=part.at[chunk(p, peer)],
                dst_ref=mbox.at[p, k - 1, :size],
                send_sem=rsend.at[p, k - 1],
                recv_sem=rrecv.at[p, k - 1],
                device_id={"cells": peer},
                device_id_type=MESH,
            )
            copy.start()
            scattered[p].append(copy)
            sends.append(copy)

    place = lax.div(me, 2)

    def spread(p, source, peer, send_sem, recv_sem):
        rows = mean.at[chunk(p, source)]
        return pltpu.make_async_remote_copy(
            src_ref=rows, dst_ref=rows, send_sem=send_sem, recv_sem=recv_sem,
            device_id={"cells": peer}, device_id_type=MESH,
        )

    def hop(p, side, j):
        sign = 1 - 2 * side
        return spread(p, me - 2 * sign * j, me + 2 * sign, gssem.at[side, p, j], grsem.at[side, p, j])

    def arrival(p, side, j):
        sign = 1 - 2 * side
        return spread(p, me - 2 * sign * j, me - 2 * sign, gssem.at[side, p, j - 1], grsem.at[side, p, j - 1])

    def handing(p, side, j):
        sign = 1 - 2 * side
        slot = side * (m - 1) + j
        return spread(p, me - 2 * sign * j, mate, fssem.at[p, slot], frsem.at[p, slot])

    def handed(p, side, j):
        sign = 1 - 2 * side
        slot = side * (m - 1) + j
        return spread(p, mate - 2 * sign * j, mate, fssem.at[p, slot], frsem.at[p, slot])

    def has(side, j):
        return place >= j if side == 0 else place + j < m

    def onward(side):
        return has(1 - side, 1)

    def reduce(p):
        size = pieces[p][1] // n
        mine = chunk(p, me)
        total = part[mine, :].astype(F32)
        for k in range(1, n):
            scattered[p][k - 1].wait_recv()
            total = total + mbox[p, k - 1, :size].astype(F32)
        mean[mine, :] = total / lon_total
        handing(p, 0, 0).start()
        for side in range(2):

            @pl.when(onward(side))
            def _():
                hop(p, side, 0).start()

    def forward(p):
        for j in range(1, m):
            for side in range(2):

                @pl.when(has(side, j))
                def _():
                    arrival(p, side, j).wait_recv()
                    handing(p, side, j).start()
                    if j < m - 1:

                        @pl.when(onward(side))
                        def _():
                            hop(p, side, j).start()

    def settle(p):
        handed(p, 0, 0).wait_recv()
        for j in range(1, m):
            for side in range(2):

                @pl.when(has(side, j))
                def _():
                    handed(p, side, j).wait_recv()

    def finish(p):
        handing(p, 0, 0).wait_send()
        for side in range(2):

            @pl.when(onward(side))
            def _():
                hop(p, side, 0).wait_send()

        for j in range(1, m):
            for side in range(2):

                @pl.when(has(side, j))
                def _():
                    handing(p, side, j).wait_send()
                    if j < m - 1:

                        @pl.when(onward(side))
                        def _():
                            hop(p, side, j).wait_send()

    def put(field, dst, block, value):
        for j in range(lons):
            cols = slice(field * width + j * LAT, field * width + (j + 1) * LAT)
            padded[dst, cols] = (block[:, j * LAT : (j + 1) * LAT].astype(F32) - value).astype(BF16)

    def anomalies(p):
        base = pieces[p][0]
        for f, ref in enumerate((geo, mer)):
            if p == 0:
                at = base + 2 * length + f * 2 * EDGE
                put(f, slice(0, EDGE), halo[f, :EDGE], mean[at : at + EDGE, :])
                end = frames + EDGE
                put(f, slice(end, end + EDGE), halo[f, EDGE:], mean[at + EDGE : at + 2 * EDGE, :])

            @pl.loop(0, length // 128)
            def _(i):
                r = pl.multiple_of(i * 128, 128)
                dst = pl.ds(pl.multiple_of(p * length + EDGE + r, 16), 128)
                put(f, dst, ref[pl.ds(p * length + r, 128), :], mean[pl.ds(base + f * length + r, 128), :])

    def filtering(p):
        tiles = length // TILE
        start = p * tiles - 1 if p else 0
        stop = (p + 1) * tiles - (0 if p == count - 1 else 1)

        @pl.loop(start, stop)
        def _(i):
            r = pl.multiple_of(i * TILE, TILE)
            for j in range(width // 256):
                a0, a1 = j * 256, (j + 1) * 256
                a = jnp.dot(taps[...], padded[pl.ds(r, SLAB), a0:a1], preferred_element_type=F32)
                b = jnp.dot(taps[...], padded[pl.ds(r, SLAB), width + a0 : width + a1], preferred_element_type=F32)
                products[pl.ds(r, TILE), a0:a1] = (a * a).astype(BF16)
                products[pl.ds(r, TILE), width + a0 : width + a1] = (b * b).astype(BF16)
                products[pl.ds(r, TILE), 2 * width + a0 : 2 * width + a1] = (a * b).astype(BF16)

    tell = []
    for t in range(count + 3):
        if t < count:
            lanes(t)
            scatter(t)
        if 1 <= t <= count:
            if t == 1:

                @pl.loop(0, frames // TILE)
                def _(i):
                    r = pl.multiple_of(i * TILE, TILE)
                    hit = lax.broadcasted_iota(jnp.int32, (DROWS, TILE), 0) == days[:, pl.ds(r, TILE)]
                    onehot[:, pl.ds(r, TILE)] = jnp.where(hit, 1.0, 0.0).astype(BF16)

                counts[...] = lax.dot_general(
                    jnp.ones((8, frames), BF16), onehot[...], (((1,), (1,)), ((), ())), preferred_element_type=F32
                )
                for k in range(1, 4):
                    copy = pltpu.make_async_remote_copy(
                        src_ref=counts, dst_ref=cbox.at[k - 1], send_sem=csem.at[k - 1], recv_sem=csem.at[2 + k],
                        device_id={"tm": lax.rem(tm + k, 4)}, device_id_type=MESH,
                    )
                    copy.start()
                    tell.append(copy)
            reduce(t - 1)
        if 2 <= t <= count + 1:
            forward(t - 2)
        if t >= 3:
            settle(t - 3)
            anomalies(t - 3)
            filtering(t - 3)

    mine = pl.ds(pl.multiple_of(core * half, 128), half)
    theirs = pl.ds(pl.multiple_of((1 - core) * half, 128), half)
    parts = [slice(s * DROWS, (s + 1) * DROWS) for s in range(3)]
    first, second, third = [], [], []
    for s, rows in enumerate(parts):
        cols = pl.ds(pl.multiple_of(s * width + (1 - core) * half, 128), half)
        give[rows, :] = jnp.dot(onehot[...], products[:, cols], preferred_element_type=F32)
        first.append(pltpu.make_async_remote_copy(
            src_ref=give.at[rows], dst_ref=inbox.at[rows], send_sem=fsem.at[s], recv_sem=fsem.at[3 + s],
            device_id={"tm": partner}, device_id_type=MESH,
        ))
        first[s].start()
    for s, rows in enumerate(parts):
        cols = pl.ds(pl.multiple_of(s * width + core * half, 128), half)
        keep[rows, :] = jnp.dot(onehot[...], products[:, cols], preferred_element_type=F32)
        first[s].wait_recv()
        own[rows, :] = (keep[rows, :] + inbox[rows, :]).astype(BF16)
        second.append(pltpu.make_async_remote_copy(
            src_ref=own.at[rows], dst_ref=other.at[rows], send_sem=ssem.at[s], recv_sem=ssem.at[3 + s],
            device_id={"tm": across}, device_id_type=MESH,
        ))
        second[s].start()
    d = lax.broadcasted_iota(jnp.int32, (DROWS, DROWS), 0)
    e = lax.broadcasted_iota(jnp.int32, (DROWS, DROWS), 1)
    gap = jnp.abs(d - e)
    inside = jnp.where(((gap <= WIN) | (gap >= DAYS - WIN)) & (e < DAYS), 1.0, 0.0).astype(F32)
    window = inside.astype(BF16)
    for rows in parts:
        inbox[rows, :] = jnp.dot(window, own[rows, :], preferred_element_type=F32)
    row = counts[0:1, :]
    for k in range(3):
        tell[k].wait()
        row = row + cbox[k, 0:1, :]
    tally = jnp.broadcast_to(jnp.sum(inside * row, axis=1, keepdims=True), (DROWS, LAT))
    for s, rows in enumerate(parts):
        second[s].wait_recv()
        total = inbox[rows, :] + jnp.dot(window, other[rows, :], preferred_element_type=F32)
        zonal_sum = jnp.zeros((DROWS, LAT), F32)
        for j in range(half // LAT):
            cols = pl.ds(pl.multiple_of(core * half + j * LAT, 128), LAT)
            value = total[:, j * LAT : (j + 1) * LAT] / tally
            climate[rows, cols] = value
            zonal_sum = zonal_sum + value
        zhalf[rows, :] = zonal_sum
        third.append(pltpu.make_async_remote_copy(
            src_ref=climate.at[rows, mine], dst_ref=climate.at[rows, mine], send_sem=tsem.at[s],
            recv_sem=tsem.at[3 + s], device_id={"tm": partner}, device_id_type=MESH,
        ))
        if s < 2:
            third[s].start()

    quarter = climate.shape[0] // 4
    swap = pltpu.make_async_remote_copy(
        src_ref=zhalf.at[pl.ds(pl.multiple_of(partner * quarter, 8), quarter)], dst_ref=zother,
        send_sem=xsem.at[0], recv_sem=xsem.at[1], device_id={"tm": partner}, device_id_type=MESH,
    )
    swap.start()
    third[2].start()
    if zrows > quarter:
        zpart[quarter:, :] = jnp.zeros((zrows - quarter, LAT), F32)
    swap.wait()
    zpart[:quarter, :] = zhalf[pl.ds(pl.multiple_of(tm * quarter, 8), quarter), :] + zother[...]
    copies = []
    for k in range(1, n):
        peer = lax.rem(me + k, n)
        copy = pltpu.make_async_remote_copy(
            src_ref=zpart.at[pl.ds(pl.multiple_of(peer * share, 8), share)],
            dst_ref=zbox.at[k - 1], send_sem=zsend.at[k - 1], recv_sem=zrecv.at[k - 1],
            device_id={"cells": peer}, device_id_type=MESH,
        )
        copy.start()
        copies.append(copy)
    block = pl.ds(pl.multiple_of(me * share, 8), share)
    total = zpart[block, :]
    for k in range(1, n):
        copies[k - 1].wait_recv()
        total = total + zbox[k - 1]
    zonal[tm, block, :] = total / lon_total
    gathers = []
    for k in range(1, n):
        copy = pltpu.make_async_remote_copy(
            src_ref=zonal.at[tm, block], dst_ref=zonal.at[tm, block],
            send_sem=gsend.at[k - 1], recv_sem=grecv.at[k - 1],
            device_id={"cells": lax.rem(me + k, n)}, device_id_type=MESH,
        )
        copy.start()
        gathers.append(copy)
    for k in range(1, n):
        copies[k - 1].wait_send()
        gathers[k - 1].wait_send()
        source = lax.rem(me + n - k, n)
        there = zonal.at[tm, pl.ds(pl.multiple_of(source * share, 8), share)]
        pltpu.make_async_remote_copy(
            src_ref=there, dst_ref=there, send_sem=gsend.at[k - 1], recv_sem=grecv.at[k - 1],
            device_id={"cells": source}, device_id_type=MESH,
        ).wait_recv()
    spreads = []
    for k in range(1, 4):
        copy = pltpu.make_async_remote_copy(
            src_ref=zonal.at[tm], dst_ref=zonal.at[tm],
            send_sem=tsend.at[k - 1], recv_sem=trecv.at[k - 1],
            device_id={"tm": lax.rem(tm + k, 4)}, device_id_type=MESH,
        )
        copy.start()
        spreads.append(copy)
    for k in range(1, 4):
        spreads[k - 1].wait_send()
        source = lax.rem(tm + 4 - k, 4)
        pltpu.make_async_remote_copy(
            src_ref=zonal.at[source], dst_ref=zonal.at[source],
            send_sem=tsend.at[k - 1], recv_sem=trecv.at[k - 1],
            device_id={"tm": source}, device_id_type=MESH,
        ).wait_recv()
    for copy in sends:
        copy.wait_send()
    for p in range(count):
        finish(p)
    for s, rows in enumerate(parts):
        first[s].wait_send()
        second[s].wait_send()
        third[s].wait_send()
        pltpu.make_async_remote_copy(
            src_ref=climate.at[rows, theirs], dst_ref=climate.at[rows, theirs], send_sem=tsem.at[s],
            recv_sem=tsem.at[3 + s], device_id={"tm": partner}, device_id_type=MESH,
        ).wait_recv()


def local(geopotential, meridional, day_index):
    frames, width = geopotential.shape
    n = lax.axis_size("cells")
    lon_total = width // LAT * n
    step = 16 * n
    count = 5
    pieces, base = [], 0
    for p in range(count):
        rows = 2 * (frames // count) + (4 * EDGE if p == 0 else 0)
        rows = -(-rows // step) * step
        pieces.append((base, rows))
        base += rows
    share = max(rows for _, rows in pieces) // n
    quarter = 3 * DROWS // 4
    zshare = -(-quarter // (8 * n)) * 8
    zrows = n * zshare
    half = width // 2

    dma = pltpu.SemaphoreType.DMA
    climate, zonal = pl.pallas_call(
        functools.partial(eddy_kernel, n, float(lon_total), zrows, pieces),
        out_shape=(
            jax.ShapeDtypeStruct((3 * DROWS, width), F32),
            jax.ShapeDtypeStruct((4, zrows, LAT), F32),
        ),
        in_specs=[pl.BlockSpec(memory_space=pl.ANY)] * 2 + [vmem()] * 2,
        out_specs=(vmem(), vmem()),
        scratch_shapes=[
            pltpu.VMEM((frames, width), BF16),
            pltpu.VMEM((frames, width), BF16),
            pltpu.VMEM((2, 2 * EDGE, width), BF16),
            pltpu.VMEM((base, LAT), BF16),
            pltpu.VMEM((count, n - 1, share, LAT), BF16),
            pltpu.VMEM((base, LAT), F32),
            pltpu.VMEM((frames + 2 * EDGE, 2 * width), BF16),
            pltpu.VMEM((frames, 3 * width), BF16),
            pltpu.VMEM((DROWS, frames), BF16),
            pltpu.VMEM((8, DROWS), F32),
            pltpu.VMEM((3 * DROWS, half), F32),
            pltpu.VMEM((3 * DROWS, half), F32),
            pltpu.VMEM((3 * DROWS, half), F32),
            pltpu.VMEM((3 * DROWS, half), BF16),
            pltpu.VMEM((3 * DROWS, half), BF16),
            pltpu.VMEM((3, 8, DROWS), F32),
            pltpu.VMEM((3 * DROWS, LAT), F32),
            pltpu.VMEM((quarter, LAT), F32),
            pltpu.VMEM((zrows, LAT), F32),
            pltpu.VMEM((n - 1, zshare, LAT), F32),
            dma((2 * count,)), dma((8,)),
            dma((count, n - 1)), dma((count, n - 1)),
            dma((2, count, n // 2 - 1)), dma((2, count, n // 2 - 1)), dma((count, n - 1)), dma((count, n - 1)),
            dma((6,)), dma((6,)), dma((6,)), dma((6,)), dma((2,)),
            dma((n - 1,)), dma((n - 1,)), dma((n - 1,)), dma((n - 1,)),
            dma((3,)), dma((3,)),
        ],
        compiler_params=pltpu.CompilerParams(collective_id=0, has_side_effects=True, vmem_limit_bytes=LIMIT),
    )(geopotential, meridional, day_index.reshape(1, frames), taps_matrix())
    climate = climate.reshape(3, DROWS, width)[:, :DAYS]
    zonal = zonal[:, :quarter].reshape(3, DROWS, LAT)[:, :DAYS]
    return (climate, zonal)


def solution(mesh):
    return jax.shard_map(
        local,
        mesh=mesh,
        in_specs=(P("tm", "cells"), P("tm", "cells"), P("tm")),
        out_specs=(P(None, None, "cells"), P()),
        check_vma=False,
    )
```

```python
import functools

import jax
import jax.numpy as jnp
import numpy as np
from jax import lax
from jax.experimental import pallas as pl
from jax.experimental.pallas import tpu as pltpu
from jax.sharding import PartitionSpec as P

LAT = 128
HALF = 15
WIN = 7
DAYS = 365
DROWS = 384
EDGE = 16
TILE = 128
SLAB = TILE + 2 * EDGE
LIMIT = 60 * 1024 * 1024
MESH = pl.DeviceIdType.MESH
F32 = jnp.float32
BF16 = jnp.bfloat16


def vmem():
    return pl.BlockSpec(memory_space=pltpu.VMEM)


def taps_matrix():
    k = np.arange(SLAB)[None, :] - np.arange(TILE)[:, None] - EDGE
    x = np.where(k == 0, 1.0, k).astype(np.float64)
    response = (np.sin(np.pi * x) - np.sin(0.25 * np.pi * x)) / (np.pi * x)
    smoother = np.sin(np.pi * x / (HALF + 1)) / (np.pi * x / (HALF + 1))
    w = np.where(k == 0, 0.75, response * smoother)
    return jnp.asarray(np.where(np.abs(k) <= HALF, w, 0.0).astype(np.float32)).astype(BF16)


def lane_sum(block):
    total = block[:, :LAT].astype(F32)
    for start in range(LAT, block.shape[1], LAT):
        total = total + block[:, start : start + LAT].astype(F32)
    return total


def eddy_kernel(
    n, lon_total, zrows, pieces, geo_in, mer_in, days, taps, climate, zonal,
    geo, mer, halo, part, mbox, mean, padded, products, onehot, counts, give, keep,
    inbox, own, other, cbox, zhalf, zother, zpart, zbox,
    lsem, hsem, rsend, rrecv, gssem, grsem, fssem, frsem,
    fsem, ssem, tsem, csem, xsem, zsend, zrecv, gsend, grecv, tsend, trecv,
):
    me = lax.axis_index("cells")
    tm = lax.axis_index("tm")
    lo = lax.rem(me, 2)
    mate = me + 1 - 2 * lo
    core = lax.rem(tm, 2)
    partner = tm + 1 - 2 * core
    across = lax.rem(tm + 2, 4)
    frames, width = geo.shape
    lons = width // LAT
    half = width // 2
    count = len(pieces)
    length = frames // count
    share = zrows // n
    m = n // 2
    barrier = pltpu.get_barrier_semaphore()
    for k in range(1, n):
        pl.semaphore_signal(barrier, inc=1, device_id={"cells": lax.rem(me + k, n)}, device_id_type=MESH)
    for k in range(1, 4):
        pl.semaphore_signal(barrier, inc=1, device_id={"tm": lax.rem(tm + k, 4)}, device_id_type=MESH)

    loads = []
    for p in range(count):
        rows = slice(p * length, (p + 1) * length)
        for f, (src, dst) in enumerate(((geo_in, geo), (mer_in, mer))):
            copy = pltpu.make_async_copy(src.at[rows], dst.at[rows], lsem.at[2 * p + f])
            copy.start()
            loads.append(copy)
    pl.semaphore_wait(barrier, n + 2)

    edges = []
    right, left = lax.rem(tm + 1, 4), lax.rem(tm + 3, 4)
    for f, ref in enumerate((geo_in, mer_in)):
        for side, (peer, start) in enumerate(((right, frames - EDGE), (left, 0))):
            slot = 2 * f + side
            copy = pltpu.make_async_remote_copy(
                src_ref=ref.at[start : start + EDGE],
                dst_ref=halo.at[f, side * EDGE : (side + 1) * EDGE],
                send_sem=hsem.at[slot],
                recv_sem=hsem.at[4 + slot],
                device_id={"tm": peer},
                device_id_type=MESH,
            )
            copy.start()
            edges.append(copy)

    sends = []
    scattered = [[] for _ in range(count)]

    def lanes(p):
        base, total_rows = pieces[p]
        loads[2 * p].wait()
        loads[2 * p + 1].wait()
        for f, ref in enumerate((geo, mer)):

            @pl.loop(0, length // 128)
            def _(i):
                r = pl.multiple_of(i * 128, 128)
                part[pl.ds(base + f * length + r, 128), :] = lane_sum(ref[pl.ds(p * length + r, 128), :]).astype(BF16)

        used = 2 * length
        if p == 0:
            for copy in edges:
                copy.wait()
            for f in range(2):
                for side, inner in enumerate((tm > 0, tm < 3)):
                    hold = jnp.where(inner, 1.0, 0.0).astype(F32)
                    dst = slice(side * EDGE, (side + 1) * EDGE)
                    halo[f, dst] = (halo[f, dst].astype(F32) * hold).astype(BF16)
                part[base + used : base + used + 2 * EDGE, :] = lane_sum(halo[f]).astype(BF16)
                used += 2 * EDGE
        if total_rows > used:
            part[base + used : base + total_rows, :] = jnp.zeros((total_rows - used, LAT), BF16)

    def chunk(p, source):
        base, total_rows = pieces[p]
        size = total_rows // n
        return pl.ds(pl.multiple_of(base + source * size, 16), size)

    def scatter(p):
        size = pieces[p][1] // n
        for k in range(1, n):
            peer = lax.rem(me + k, n)
            copy = pltpu.make_async_remote_copy(
                src_ref=part.at[chunk(p, peer)],
                dst_ref=mbox.at[p, k - 1, :size],
                send_sem=rsend.at[p, k - 1],
                recv_sem=rrecv.at[p, k - 1],
                device_id={"cells": peer},
                device_id_type=MESH,
            )
            copy.start()
            scattered[p].append(copy)
            sends.append(copy)

    place = lax.div(me, 2)

    def spread(p, source, peer, send_sem, recv_sem):
        rows = mean.at[chunk(p, source)]
        return pltpu.make_async_remote_copy(
            src_ref=rows, dst_ref=rows, send_sem=send_sem, recv_sem=recv_sem,
            device_id={"cells": peer}, device_id_type=MESH,
        )

    def hop(p, side, j):
        sign = 1 - 2 * side
        return spread(p, me - 2 * sign * j, me + 2 * sign, gssem.at[side, p, j], grsem.at[side, p, j])

    def arrival(p, side, j):
        sign = 1 - 2 * side
        return spread(p, me - 2 * sign * j, me - 2 * sign, gssem.at[side, p, j - 1], grsem.at[side, p, j - 1])

    def handing(p, side, j):
        sign = 1 - 2 * side
        slot = side * (m - 1) + j
        return spread(p, me - 2 * sign * j, mate, fssem.at[p, slot], frsem.at[p, slot])

    def handed(p, side, j):
        sign = 1 - 2 * side
        slot = side * (m - 1) + j
        return spread(p, mate - 2 * sign * j, mate, fssem.at[p, slot], frsem.at[p, slot])

    def has(side, j):
        return place >= j if side == 0 else place + j < m

    def onward(side):
        return has(1 - side, 1)

    def reduce(p):
        size = pieces[p][1] // n
        mine = chunk(p, me)
        total = part[mine, :].astype(F32)
        for k in range(1, n):
            scattered[p][k - 1].wait_recv()
            total = total + mbox[p, k - 1, :size].astype(F32)
        mean[mine, :] = total / lon_total
        handing(p, 0, 0).start()
        for side in range(2):

            @pl.when(onward(side))
            def _():
                hop(p, side, 0).start()

    def forward(p):
        for j in range(1, m):
            for side in range(2):

                @pl.when(has(side, j))
                def _():
                    arrival(p, side, j).wait_recv()
                    handing(p, side, j).start()
                    if j < m - 1:

                        @pl.when(onward(side))
                        def _():
                            hop(p, side, j).start()

    def settle(p):
        handed(p, 0, 0).wait_recv()
        for j in range(1, m):
            for side in range(2):

                @pl.when(has(side, j))
                def _():
                    handed(p, side, j).wait_recv()

    def finish(p):
        handing(p, 0, 0).wait_send()
        for side in range(2):

            @pl.when(onward(side))
            def _():
                hop(p, side, 0).wait_send()

        for j in range(1, m):
            for side in range(2):

                @pl.when(has(side, j))
                def _():
                    handing(p, side, j).wait_send()
                    if j < m - 1:

                        @pl.when(onward(side))
                        def _():
                            hop(p, side, j).wait_send()

    def put(field, dst, block, value):
        for j in range(lons):
            cols = slice(field * width + j * LAT, field * width + (j + 1) * LAT)
            padded[dst, cols] = (block[:, j * LAT : (j + 1) * LAT].astype(F32) - value).astype(BF16)

    def anomalies(p):
        base = pieces[p][0]
        for f, ref in enumerate((geo, mer)):
            if p == 0:
                at = base + 2 * length + f * 2 * EDGE
                put(f, slice(0, EDGE), halo[f, :EDGE], mean[at : at + EDGE, :])
                end = frames + EDGE
                put(f, slice(end, end + EDGE), halo[f, EDGE:], mean[at + EDGE : at + 2 * EDGE, :])

            @pl.loop(0, length // 128)
            def _(i):
                r = pl.multiple_of(i * 128, 128)
                dst = pl.ds(pl.multiple_of(p * length + EDGE + r, 16), 128)
                put(f, dst, ref[pl.ds(p * length + r, 128), :], mean[pl.ds(base + f * length + r, 128), :])

    def filtering(p):
        tiles = length // TILE
        start = p * tiles - 1 if p else 0
        stop = (p + 1) * tiles - (0 if p == count - 1 else 1)

        @pl.loop(start, stop)
        def _(i):
            r = pl.multiple_of(i * TILE, TILE)
            for j in range(width // 256):
                a0, a1 = j * 256, (j + 1) * 256
                a = jnp.dot(taps[...], padded[pl.ds(r, SLAB), a0:a1], preferred_element_type=F32)
                b = jnp.dot(taps[...], padded[pl.ds(r, SLAB), width + a0 : width + a1], preferred_element_type=F32)
                products[pl.ds(r, TILE), a0:a1] = (a * a).astype(BF16)
                products[pl.ds(r, TILE), width + a0 : width + a1] = (b * b).astype(BF16)
                products[pl.ds(r, TILE), 2 * width + a0 : 2 * width + a1] = (a * b).astype(BF16)

    tell = []
    for t in range(count + 4):
        if t < count:
            lanes(t)
            scatter(t)
        if 2 <= t <= count + 1:
            if t == 2:

                @pl.loop(0, frames // TILE)
                def _(i):
                    r = pl.multiple_of(i * TILE, TILE)
                    hit = lax.broadcasted_iota(jnp.int32, (DROWS, TILE), 0) == days[:, pl.ds(r, TILE)]
                    onehot[:, pl.ds(r, TILE)] = jnp.where(hit, 1.0, 0.0).astype(BF16)

                counts[...] = lax.dot_general(
                    jnp.ones((8, frames), BF16), onehot[...], (((1,), (1,)), ((), ())), preferred_element_type=F32
                )
                for k in range(1, 4):
                    copy = pltpu.make_async_remote_copy(
                        src_ref=counts, dst_ref=cbox.at[k - 1], send_sem=csem.at[k - 1], recv_sem=csem.at[2 + k],
                        device_id={"tm": lax.rem(tm + k, 4)}, device_id_type=MESH,
                    )
                    copy.start()
                    tell.append(copy)
            reduce(t - 2)
        if 3 <= t <= count + 2:
            forward(t - 3)
        if t >= 4:
            settle(t - 4)
            anomalies(t - 4)
            filtering(t - 4)

    mine = pl.ds(pl.multiple_of(core * half, 128), half)
    theirs = pl.ds(pl.multiple_of((1 - core) * half, 128), half)
    parts = [slice(s * DROWS, (s + 1) * DROWS) for s in range(3)]
    first, second, third = [], [], []

    def hand_over(s):
        rows = parts[s]
        cols = pl.ds(pl.multiple_of(s * width + (1 - core) * half, 128), half)
        give[rows, :] = jnp.dot(onehot[...], products[:, cols], preferred_element_type=F32)
        first.append(pltpu.make_async_remote_copy(
            src_ref=give.at[rows], dst_ref=inbox.at[rows], send_sem=fsem.at[s], recv_sem=fsem.at[3 + s],
            device_id={"tm": partner}, device_id_type=MESH,
        ))
        first[s].start()

    hand_over(0)
    for s, rows in enumerate(parts):
        cols = pl.ds(pl.multiple_of(s * width + core * half, 128), half)
        keep[rows, :] = jnp.dot(onehot[...], products[:, cols], preferred_element_type=F32)
        if s < 2:
            hand_over(s + 1)
        first[s].wait_recv()
        own[rows, :] = (keep[rows, :] + inbox[rows, :]).astype(BF16)
        second.append(pltpu.make_async_remote_copy(
            src_ref=own.at[rows], dst_ref=other.at[rows], send_sem=ssem.at[s], recv_sem=ssem.at[3 + s],
            device_id={"tm": across}, device_id_type=MESH,
        ))
        second[s].start()
    d = lax.broadcasted_iota(jnp.int32, (DROWS, DROWS), 0)
    e = lax.broadcasted_iota(jnp.int32, (DROWS, DROWS), 1)
    gap = jnp.abs(d - e)
    inside = jnp.where(((gap <= WIN) | (gap >= DAYS - WIN)) & (e < DAYS), 1.0, 0.0).astype(F32)
    window = inside.astype(BF16)
    for rows in parts:
        inbox[rows, :] = jnp.dot(window, own[rows, :], preferred_element_type=F32)
    row = counts[0:1, :]
    for k in range(3):
        tell[k].wait()
        row = row + cbox[k, 0:1, :]
    tally = jnp.broadcast_to(jnp.sum(inside * row, axis=1, keepdims=True), (DROWS, LAT))
    for s, rows in enumerate(parts):
        second[s].wait_recv()
        total = inbox[rows, :] + jnp.dot(window, other[rows, :], preferred_element_type=F32)
        zonal_sum = jnp.zeros((DROWS, LAT), F32)
        for j in range(half // LAT):
            cols = pl.ds(pl.multiple_of(core * half + j * LAT, 128), LAT)
            value = total[:, j * LAT : (j + 1) * LAT] / tally
            climate[rows, cols] = value
            zonal_sum = zonal_sum + value
        zhalf[rows, :] = zonal_sum
        third.append(pltpu.make_async_remote_copy(
            src_ref=climate.at[rows, mine], dst_ref=climate.at[rows, mine], send_sem=tsem.at[s],
            recv_sem=tsem.at[3 + s], device_id={"tm": partner}, device_id_type=MESH,
        ))
        if s < 2:
            third[s].start()

    quarter = climate.shape[0] // 4
    swap = pltpu.make_async_remote_copy(
        src_ref=zhalf.at[pl.ds(pl.multiple_of(partner * quarter, 8), quarter)], dst_ref=zother,
        send_sem=xsem.at[0], recv_sem=xsem.at[1], device_id={"tm": partner}, device_id_type=MESH,
    )
    swap.start()
    third[2].start()
    if zrows > quarter:
        zpart[quarter:, :] = jnp.zeros((zrows - quarter, LAT), F32)
    swap.wait()
    zpart[:quarter, :] = zhalf[pl.ds(pl.multiple_of(tm * quarter, 8), quarter), :] + zother[...]
    copies = []
    for k in range(1, n):
        peer = lax.rem(me + k, n)
        copy = pltpu.make_async_remote_copy(
            src_ref=zpart.at[pl.ds(pl.multiple_of(peer * share, 8), share)],
            dst_ref=zbox.at[k - 1], send_sem=zsend.at[k - 1], recv_sem=zrecv.at[k - 1],
            device_id={"cells": peer}, device_id_type=MESH,
        )
        copy.start()
        copies.append(copy)
    block = pl.ds(pl.multiple_of(me * share, 8), share)
    total = zpart[block, :]
    for k in range(1, n):
        copies[k - 1].wait_recv()
        total = total + zbox[k - 1]
    zonal[tm, block, :] = total / lon_total
    gathers = []
    for k in range(1, n):
        copy = pltpu.make_async_remote_copy(
            src_ref=zonal.at[tm, block], dst_ref=zonal.at[tm, block],
            send_sem=gsend.at[k - 1], recv_sem=grecv.at[k - 1],
            device_id={"cells": lax.rem(me + k, n)}, device_id_type=MESH,
        )
        copy.start()
        gathers.append(copy)
    for k in range(1, n):
        copies[k - 1].wait_send()
        gathers[k - 1].wait_send()
        source = lax.rem(me + n - k, n)
        there = zonal.at[tm, pl.ds(pl.multiple_of(source * share, 8), share)]
        pltpu.make_async_remote_copy(
            src_ref=there, dst_ref=there, send_sem=gsend.at[k - 1], recv_sem=grecv.at[k - 1],
            device_id={"cells": source}, device_id_type=MESH,
        ).wait_recv()
    spreads = []
    for k in range(1, 4):
        copy = pltpu.make_async_remote_copy(
            src_ref=zonal.at[tm], dst_ref=zonal.at[tm],
            send_sem=tsend.at[k - 1], recv_sem=trecv.at[k - 1],
            device_id={"tm": lax.rem(tm + k, 4)}, device_id_type=MESH,
        )
        copy.start()
        spreads.append(copy)
    for k in range(1, 4):
        spreads[k - 1].wait_send()
        source = lax.rem(tm + 4 - k, 4)
        pltpu.make_async_remote_copy(
            src_ref=zonal.at[source], dst_ref=zonal.at[source],
            send_sem=tsend.at[k - 1], recv_sem=trecv.at[k - 1],
            device_id={"tm": source}, device_id_type=MESH,
        ).wait_recv()
    for copy in sends:
        copy.wait_send()
    for p in range(count):
        finish(p)
    for s, rows in enumerate(parts):
        first[s].wait_send()
        second[s].wait_send()
        third[s].wait_send()
        pltpu.make_async_remote_copy(
            src_ref=climate.at[rows, theirs], dst_ref=climate.at[rows, theirs], send_sem=tsem.at[s],
            recv_sem=tsem.at[3 + s], device_id={"tm": partner}, device_id_type=MESH,
        ).wait_recv()


def local(geopotential, meridional, day_index):
    frames, width = geopotential.shape
    n = lax.axis_size("cells")
    lon_total = width // LAT * n
    step = 16 * n
    count = 5
    pieces, base = [], 0
    for p in range(count):
        rows = 2 * (frames // count) + (4 * EDGE if p == 0 else 0)
        rows = -(-rows // step) * step
        pieces.append((base, rows))
        base += rows
    share = max(rows for _, rows in pieces) // n
    quarter = 3 * DROWS // 4
    zshare = -(-quarter // (8 * n)) * 8
    zrows = n * zshare
    half = width // 2

    dma = pltpu.SemaphoreType.DMA
    climate, zonal = pl.pallas_call(
        functools.partial(eddy_kernel, n, float(lon_total), zrows, pieces),
        out_shape=(
            jax.ShapeDtypeStruct((3 * DROWS, width), F32),
            jax.ShapeDtypeStruct((4, zrows, LAT), F32),
        ),
        in_specs=[pl.BlockSpec(memory_space=pl.ANY)] * 2 + [vmem()] * 2,
        out_specs=(vmem(), vmem()),
        scratch_shapes=[
            pltpu.VMEM((frames, width), BF16),
            pltpu.VMEM((frames, width), BF16),
            pltpu.VMEM((2, 2 * EDGE, width), BF16),
            pltpu.VMEM((base, LAT), BF16),
            pltpu.VMEM((count, n - 1, share, LAT), BF16),
            pltpu.VMEM((base, LAT), F32),
            pltpu.VMEM((frames + 2 * EDGE, 2 * width), BF16),
            pltpu.VMEM((frames, 3 * width), BF16),
            pltpu.VMEM((DROWS, frames), BF16),
            pltpu.VMEM((8, DROWS), F32),
            pltpu.VMEM((3 * DROWS, half), F32),
            pltpu.VMEM((3 * DROWS, half), F32),
            pltpu.VMEM((3 * DROWS, half), F32),
            pltpu.VMEM((3 * DROWS, half), BF16),
            pltpu.VMEM((3 * DROWS, half), BF16),
            pltpu.VMEM((3, 8, DROWS), F32),
            pltpu.VMEM((3 * DROWS, LAT), F32),
            pltpu.VMEM((quarter, LAT), F32),
            pltpu.VMEM((zrows, LAT), F32),
            pltpu.VMEM((n - 1, zshare, LAT), F32),
            dma((2 * count,)), dma((8,)),
            dma((count, n - 1)), dma((count, n - 1)),
            dma((2, count, n // 2 - 1)), dma((2, count, n // 2 - 1)), dma((count, n - 1)), dma((count, n - 1)),
            dma((6,)), dma((6,)), dma((6,)), dma((6,)), dma((2,)),
            dma((n - 1,)), dma((n - 1,)), dma((n - 1,)), dma((n - 1,)),
            dma((3,)), dma((3,)),
        ],
        compiler_params=pltpu.CompilerParams(collective_id=0, has_side_effects=True, vmem_limit_bytes=LIMIT),
    )(geopotential, meridional, day_index.reshape(1, frames), taps_matrix())
    climate = climate.reshape(3, DROWS, width)[:, :DAYS]
    zonal = zonal[:, :quarter].reshape(3, DROWS, LAT)[:, :DAYS]
    return (climate, zonal)


def solution(mesh):
    return jax.shard_map(
        local,
        mesh=mesh,
        in_specs=(P("tm", "cells"), P("tm", "cells"), P("tm")),
        out_specs=(P(None, None, "cells"), P()),
        check_vma=False,
    )
```
